128 devices in a mesh: face: 8 (over z_lo, x), tile: 16 (over z_hi, y, core).
Axes of the slice: x: 4, y: 4, z: 4 (z_hi: 2, z_lo: 2; z = z_hi * 2 + z_lo), core: 2. Of those that a mesh axis runs over, the one named last changes fastest.
Arguments:
- source: bfloat16 [8192, 16, 128], P(('face', 'tile')), may hold values from -6 to 6
- entry_block: int32 [16384], P(('face', 'tile')), may hold values from 0 to 16383, as said below
- entry_source: int32 [16384], P(('face', 'tile')), may hold values from 0 to 63
- entry_weight: bfloat16 [16384, 128, 128], P(('face', 'tile')), may hold values from -0.5 to 0.5
- lat_to_nested: int32 [16384], P(('face', 'tile')), may hold values from 0 to 16383, as said below
- face_links: int32 [8, 4, 3], replicated, may hold values from 0 to 7, as said below
- w_in: bfloat16 [16, 90], replicated, may hold values from -1.5 to 1.5
- b_in: float32 [90], replicated, may hold values from -3 to 3
- kernel: float32 [9, 90], replicated, may hold values from -2 to 2
- ln_gain: float32 [90], replicated, may hold values from 0.1 to 1.9
- ln_bias: float32 [90], replicated, may hold values from -3 to 3
- w_one: bfloat16 [90, 360], replicated, may hold values from -0.625 to 0.625
- b_one: float32 [360], replicated, may hold values from -3 to 3
- w_two: bfloat16 [360, 90], replicated, may hold values from -0.3125 to 0.3125
- b_two: float32 [90], replicated, may hold values from -3 to 3
- cotangent: bfloat16 [8, 90, 512, 512], P('face', None, 'tile'), may hold values from -6 to 6
Outputs:
- output: bfloat16 [8, 90, 512, 512], P('face', None, 'tile')
- grad_one: float32 [90, 360], replicated
- grad_two: float32 [360, 90], replicated
- grad_kernel: float32 [9, 90], replicated
The draws below stay inside these ranges and needn't reach their ends.
Inputs may be any that keep to these rules, and one draw needn't show every extreme that they name: `entry_block`: blocks k * 128 to (k + 1) * 128 - 1 belong to device k. At most 2 entries of one device name blocks of one device; in every draw one device gets exactly 2 from every device. `lat_to_nested`: A permutation of all blocks; the 128 blocks of each device go one to each device. `face_links`: entry [f, s, 0] names a face other than f; [f, s, 1] a side 0 to 3; [f, s, 2] is 0 or 1.
All inputs are finite; a program needn't handle non-finite values.
Results may differ from the reference program's by a relative error of at most 0.0081.
Values may be sent and summed in bfloat16 or wider, within the bound.
A program may use at most 192 MiB of HBM per device.

```python
import math
import jax
import jax.numpy as jnp
from jax import lax

IN_CH = 16
LATENT = 90
HIDDEN_SIZE = 360
ROWS_DEV = 32
SRC_DEV = 64
SB = 128
CAP = 2
NSIDE = 512
FACES = 8
RB_DEV = 128
PB = 128
E_DEV = 128
DEVICES = 128


def draw_entry_block(key, part):
    key_hot, key_rest, key_local = jax.random.split(key, 3)
    hot_dev = jax.random.randint(key_hot, (), 0, DEVICES).astype(jnp.int32)

    def one_source(sub_key):
        slot_order = jax.random.permutation(sub_key, (DEVICES - 1) * CAP)
        pick_dev = (slot_order[:E_DEV - CAP] // CAP).astype(jnp.int32)
        others = pick_dev + (pick_dev >= hot_dev).astype(jnp.int32)
        return jnp.concatenate([jnp.full((CAP,), 0, jnp.int32) + hot_dev, others])
    owners = jax.vmap(one_source)(jax.random.split(key_rest, DEVICES))
    local_ids = jax.random.randint(key_local, (DEVICES, E_DEV), 0, RB_DEV).astype(jnp.int32)
    return (owners * RB_DEV + local_ids).reshape(DEVICES * E_DEV).astype(jnp.int32)


def draw_lat_to_nested(key, part):
    key_send, key_place = jax.random.split(key)
    send_dev = jax.vmap(lambda sub_key: jax.random.permutation(sub_key, RB_DEV))(jax.random.split(key_send, DEVICES)).astype(jnp.int32)
    slot_table = jax.vmap(lambda sub_key: jax.random.permutation(sub_key, DEVICES))(jax.random.split(key_place, DEVICES)).astype(jnp.int32)
    source_ids = jnp.broadcast_to(jnp.arange(DEVICES, dtype=jnp.int32)[:, None], send_dev.shape)
    slot_pos = slot_table[send_dev, source_ids]
    return (send_dev * RB_DEV + slot_pos).reshape(DEVICES * RB_DEV).astype(jnp.int32)


def draw_face_links(key, part):
    key_face, key_side, key_flip = jax.random.split(key, 3)
    offset = jax.random.randint(key_face, (FACES, 4), 1, FACES)
    neighbour = (jnp.arange(FACES, dtype=jnp.int32)[:, None] + offset) % FACES
    which_side = jax.random.randint(key_side, (FACES, 4), 0, 4)
    flipped = jax.random.randint(key_flip, (FACES, 4), 0, 2)
    return jnp.stack([neighbour, which_side, flipped], axis=2).astype(jnp.int32)


def place_ends(result, stream_key, low, largest):
    extent = result.shape
    spot = [jax.random.randint(jax.random.fold_in(stream_key, axis), (), 0, extent[axis]) for axis in range(len(extent))]
    result = result.at[tuple(spot)].set(low)
    longest = extent.index(max(extent))
    spot[longest] = (spot[longest] + 1) % extent[longest]
    return result.at[tuple(spot)].set(largest)


def block_scale(own_key, dims, cuts, least, top_value):
    def one(axis_at, shards_of):
        heights = jax.random.uniform(jax.random.fold_in(jax.random.fold_in(own_key, 6), axis_at), (shards_of,), jnp.float32, least / len(cuts), top_value / len(cuts))
        return jnp.repeat(jnp.exp(heights), dims[axis_at] // shards_of).reshape((-1,) + (1,) * (len(dims) - axis_at - 1))

    factor_of = one(*cuts[0])
    for cut in cuts[1:]:
        factor_of = factor_of * one(*cut)
    return factor_of


def bell_draw(own_key, extent, width, reach, cuts=(), kind=jnp.bfloat16):
    gain = block_scale(own_key, extent, cuts, -0.22, 0.18) if cuts else 1.0
    entries = jax.random.normal(own_key, extent, jnp.float32) * width * gain
    return jnp.minimum(jnp.maximum(entries, -reach), reach).astype(kind)


def setup_inputs(seed: int = 0) -> dict:
    keys = jax.random.split(jax.random.key(seed), 17)
    source = bell_draw(keys[0], (DEVICES * SRC_DEV, IN_CH, SB), 1.0, 6.0, ((0, 128),))
    entry_block = draw_entry_block(jax.random.fold_in(keys[16], 71), 0)
    entry_source = place_ends(jax.random.randint(keys[2], (DEVICES * E_DEV,), 0, SRC_DEV), jax.random.fold_in(keys[2], 1), 0, SRC_DEV - 1).astype(jnp.int32)
    entry_weight = bell_draw(keys[3], (DEVICES * E_DEV, SB, PB), SB ** -0.5, 0.5, ((0, 128),))
    lat_to_nested = draw_lat_to_nested(jax.random.fold_in(keys[16], 71), 0)
    face_links = draw_face_links(jax.random.fold_in(keys[16], 71), 0)
    w_in = bell_draw(keys[6], (IN_CH, LATENT), IN_CH ** -0.5, 1.5)
    b_in = bell_draw(keys[7], (LATENT,), 0.5, 3.0, (), jnp.float32)
    kernel = bell_draw(keys[8], (9, LATENT), 9 ** -0.5, 2.0, (), jnp.float32)
    ln_gain = jnp.clip(1.0 + 0.18 * jax.random.normal(keys[9], (LATENT,), jnp.float32), 0.1, 1.9)
    ln_bias = bell_draw(keys[10], (LATENT,), 0.5, 3.0, (), jnp.float32)
    w_one = bell_draw(keys[11], (LATENT, HIDDEN_SIZE), LATENT ** -0.5, 0.625)
    b_one = bell_draw(keys[12], (HIDDEN_SIZE,), 0.5, 3.0, (), jnp.float32)
    w_two = bell_draw(keys[13], (HIDDEN_SIZE, LATENT), HIDDEN_SIZE ** -0.5, 0.3125)
    b_two = bell_draw(keys[14], (LATENT,), 0.5, 3.0, (), jnp.float32)
    cotangent = bell_draw(keys[15], (FACES, LATENT, NSIDE, NSIDE), 1.0, 6.0, ((0, 8), (2, 16)))
    return dict(source=source, entry_block=entry_block, entry_source=entry_source, entry_weight=entry_weight, lat_to_nested=lat_to_nested, face_links=face_links, w_in=w_in, b_in=b_in, kernel=kernel, ln_gain=ln_gain, ln_bias=ln_bias, w_one=w_one, b_one=b_one, w_two=w_two, b_two=b_two, cotangent=cotangent)


GELU_K = 0.7978845608028654
GELU_C = 0.044715
NORM_EPS = 1e-06

def gelu_pair(pre_act):
    inner = GELU_K * (pre_act + GELU_C * pre_act * pre_act * pre_act)
    tanh_val = jnp.tanh(inner)
    gelu_val = 0.5 * pre_act * (1.0 + tanh_val)
    gelu_slope = 0.5 * (1.0 + tanh_val) + 0.5 * pre_act * (1.0 - tanh_val * tanh_val) * GELU_K * (1.0 + 3.0 * GELU_C * pre_act * pre_act)
    return (gelu_val, gelu_slope)

def contract_rows(left_mat, right_mat):
    return lax.dot_general(left_mat, right_mat, (((1,), (1,)), ((), ())), preferred_element_type=jnp.float32)

def strip_work(padded, middle, cotan, kernel, ln_gain, ln_bias, w_one, b_one, w_two, b_two, scale):
    lat_count = padded.shape[0]
    row_count = padded.shape[1] - 2
    col_count = padded.shape[2] - 2
    wide = padded.astype(jnp.float32)
    depth_sum = jnp.zeros((lat_count, row_count, col_count), jnp.float32)
    for tap_index in range(9):
        row_off = tap_index // 3
        col_off = tap_index % 3
        window = wide[:, row_off:row_off + row_count, col_off:col_off + col_count]
        depth_sum = depth_sum + kernel[tap_index][:, None, None] * window
    flat = depth_sum.reshape(lat_count, row_count * col_count)
    mean_val = lax.optimization_barrier(jnp.mean(flat, axis=0, keepdims=True))
    centered = flat - mean_val
    variance = lax.optimization_barrier(jnp.mean(centered * centered, axis=0, keepdims=True))
    inv_std = lax.rsqrt(variance + NORM_EPS)
    scaled = centered * inv_std
    normed = (scaled * ln_gain[:, None] + ln_bias[:, None]).astype(jnp.bfloat16)
    pre_act = jnp.dot(w_one.T, normed, preferred_element_type=jnp.float32) + b_one[:, None]
    gelu_val, gelu_slope = gelu_pair(pre_act)
    hidden = gelu_val.astype(jnp.bfloat16)
    summed = jnp.dot(w_two.T, hidden, preferred_element_type=jnp.float32) + b_two[:, None] + middle.reshape(lat_count, -1).astype(jnp.float32)
    output = summed.astype(jnp.bfloat16).reshape(lat_count, row_count, col_count)
    cot_flat = cotan.reshape(lat_count, -1)
    grad_two = contract_rows(hidden, cot_flat) * scale
    back_hidden = jnp.dot(w_two, cot_flat, preferred_element_type=jnp.float32)
    back_pre = (back_hidden * gelu_slope).astype(jnp.bfloat16)
    grad_one = contract_rows(normed, back_pre) * scale
    back_hat = jnp.dot(w_one, back_pre, preferred_element_type=jnp.float32) * ln_gain[:, None]
    back_depth = inv_std * (back_hat - lax.optimization_barrier(jnp.mean(back_hat, axis=0, keepdims=True)) - scaled * lax.optimization_barrier(jnp.mean(back_hat * scaled, axis=0, keepdims=True)))
    back_grid = back_depth.reshape(lat_count, row_count, col_count)
    kernel_rows = []
    for tap_index in range(9):
        row_off = tap_index // 3
        col_off = tap_index % 3
        window = wide[:, row_off:row_off + row_count, col_off:col_off + col_count]
        kernel_rows.append(lax.optimization_barrier(jnp.sum(back_grid * window, axis=(1, 2))))
    grad_kernel = jnp.stack(kernel_rows, axis=0) * scale
    return (output, grad_one, grad_two, grad_kernel)

def reference(source, entry_block, entry_source, entry_weight, lat_to_nested, face_links, w_in, b_in, kernel, ln_gain, ln_bias, w_one, b_one, w_two, b_two, cotangent):
    sources = source.reshape(DEVICES, SRC_DEV, IN_CH, SB)
    weights = entry_weight.reshape(DEVICES, E_DEV, SB, PB)
    pick_ids = entry_source.reshape(DEVICES, E_DEV)

    def device_partials(packed):
        own_source, own_weight, own_pick = packed
        chosen = jnp.take(own_source, own_pick, axis=0).astype(jnp.float32)
        return jnp.einsum('eis,esp->eip', chosen, own_weight.astype(jnp.float32)).astype(jnp.bfloat16)
    partials = lax.map(device_partials, (sources, weights, pick_ids))
    flat_parts = partials.reshape(DEVICES * E_DEV, IN_CH, PB).astype(jnp.float32)
    lat_field = jnp.zeros((DEVICES * RB_DEV, IN_CH, PB), jnp.float32).at[entry_block].add(flat_parts).astype(jnp.bfloat16)
    nested = jnp.zeros_like(lat_field).at[lat_to_nested].set(lat_field)
    strip_count = NSIDE // ROWS_DEV
    in_grid = nested.reshape(FACES, strip_count, RB_DEV, IN_CH, PB).transpose(0, 3, 1, 2, 4).reshape(FACES, IN_CH, NSIDE, NSIDE)

    def lift_face(face_in):
        mixed = jnp.dot(w_in.T, face_in.reshape(IN_CH, -1), preferred_element_type=jnp.float32) + b_in[:, None]
        return mixed.astype(jnp.bfloat16).reshape(LATENT, NSIDE, NSIDE)
    latent = lax.map(lift_face, in_grid)
    all_lines = jnp.stack([latent[:, :, 0, :], latent[:, :, NSIDE - 1, :], latent[:, :, :, 0], latent[:, :, :, NSIDE - 1]], axis=1)
    scale = 1.0 / math.sqrt(FACES * NSIDE * NSIDE)
    zero_grads = (jnp.zeros((LATENT, HIDDEN_SIZE), jnp.float32), jnp.zeros((HIDDEN_SIZE, LATENT), jnp.float32), jnp.zeros((9, LATENT), jnp.float32))

    def one_face(face_idx):
        face_link = face_links[face_idx]
        picked = all_lines[face_link[:, 0], face_link[:, 1]]
        picked = jnp.where(face_link[:, 2][:, None, None] == 1, picked[:, :, ::-1], picked)
        face_field = latent[face_idx]
        padded = jnp.zeros((LATENT, NSIDE + 2, NSIDE + 2), jnp.bfloat16)
        padded = padded.at[:, 1:NSIDE + 1, 1:NSIDE + 1].set(face_field)
        padded = padded.at[:, 0, 1:NSIDE + 1].set(picked[0])
        padded = padded.at[:, NSIDE + 1, 1:NSIDE + 1].set(picked[1])
        padded = padded.at[:, 1:NSIDE + 1, 0].set(picked[2])
        padded = padded.at[:, 1:NSIDE + 1, NSIDE + 1].set(picked[3])
        face_cot = cotangent[face_idx]

        def strip_step(carry, strip_idx):
            row_start = (strip_idx * ROWS_DEV).astype(jnp.int32)
            block = lax.dynamic_slice_in_dim(padded, row_start, ROWS_DEV + 2, 1)
            middle = lax.dynamic_slice_in_dim(face_field, row_start, ROWS_DEV, 1)
            cotan = lax.dynamic_slice_in_dim(face_cot, row_start, ROWS_DEV, 1)
            output, grad_one, grad_two, grad_kernel = strip_work(block, middle, cotan, kernel, ln_gain, ln_bias, w_one, b_one, w_two, b_two, scale)
            return ((carry[0] + grad_one, carry[1] + grad_two, carry[2] + grad_kernel), output)
        totals, pieces = lax.scan(strip_step, zero_grads, jnp.arange(strip_count, dtype=jnp.int32))
        return (pieces.transpose(1, 0, 2, 3).reshape(LATENT, NSIDE, NSIDE), totals)
    outputs, face_totals = lax.map(one_face, jnp.arange(FACES, dtype=jnp.int32))
    return (outputs, lax.optimization_barrier(jnp.sum(face_totals[0], axis=0)), lax.optimization_barrier(jnp.sum(face_totals[1], axis=0)), lax.optimization_barrier(jnp.sum(face_totals[2], axis=0)))
```

```python
import functools
import math

import jax
import jax.numpy as jnp
from jax import lax
from jax.experimental import pallas as pl
from jax.experimental.pallas import tpu as pltpu
from jax.sharding import PartitionSpec as P


GELU_K = 0.7978845608028654
GELU_C = 0.044715
NORM_EPS = 1e-06
CP = 96
HP = 368
UNROLL = 2
MIB = 1024 * 1024


def strip_kernel(
    inv_ref, flag_ref, blocks_ref, rows_ref, cols_ref, cot_ref, win_ref, vec_ref, kern_ref, w1t_ref, w2t_ref, w1_ref,
    w2_ref, out_ref, grad_ref, field, cols, cot_s, out_s, depth_s, scaled_s, norm_s, cotb_s, pre_s, back_s, hid_s, bp_s,
    bd_s, g2_s, g1_s, gk_s, scale,
):
    chans, rows, width = cot_ref.shape
    lanes = width // 128
    f32 = jnp.float32
    bf16 = jnp.bfloat16

    def wide(v):
        return jnp.concatenate([v] * lanes, axis=1)

    def lift(x):
        return (jnp.dot(win_ref[...], x, preferred_element_type=f32)).astype(bf16)

    b_in = vec_ref[0]
    lane = lax.broadcasted_iota(jnp.int32, (CP, 128), 1)
    last = lane == jnp.where(flag_ref[1] == 1, rows + 1, -1)
    first = lane == jnp.where(flag_ref[0] == 1, 0, -1)
    for side in range(2):
        v = jnp.dot(win_ref[...], cols_ref[side], preferred_element_type=f32) + b_in
        v = v.astype(bf16).astype(f32)
        cols[side] = jnp.where(first | last, 0.0, v)

    g2_s[...] = jnp.zeros_like(g2_s)
    g1_s[...] = jnp.zeros_like(g1_s)
    gk_s[...] = jnp.zeros_like(gk_s)
    cot_s[:, chans * rows :, :] = jnp.zeros((lanes, (CP - chans) * rows, 128), f32)

    def turn(c, _):
        x = cot_ref[c].astype(f32)
        for k in range(lanes):
            cot_s[k, pl.ds(pl.multiple_of(c * rows, rows), rows), :] = x[:, k * 128 : (k + 1) * 128]
        return 0

    lax.fori_loop(0, chans, turn, 0)

    def make_row(at, x):
        lat = jnp.dot(win_ref[...], x, preferred_element_type=f32) + wide(b_in)
        lat = lat.astype(bf16).astype(f32)
        wide_lane = lax.broadcasted_iota(jnp.int32, (CP, width), 1)
        left = wide(pltpu.roll(cols[0], lax.rem(128 - at, 128), 1))
        right = wide(pltpu.roll(cols[1], 127 - at, 1))
        field[at, 0] = jnp.where(wide_lane == 0, left, pltpu.roll(lat, 1, 1))
        field[at, 1] = lat
        field[at, 2] = jnp.where(wide_lane == width - 1, right, pltpu.roll(lat, width - 1, 1))

    def row_of(r):
        return jnp.concatenate([blocks_ref[inv_ref[r * lanes + k]] for k in range(lanes)], axis=1)

    make_row(0, jnp.concatenate([rows_ref[0, k] for k in range(lanes)], axis=1))
    make_row(rows + 1, jnp.concatenate([rows_ref[1, k] for k in range(lanes)], axis=1))
    make_row(1, row_of(0))

    lane_w = lax.broadcasted_iota(jnp.int32, (8, width), 0)
    tail = (lane_w < chans - (CP - 8)).astype(f32)
    ones_rows = (lane_w == chans - (CP - 8)) | (lane_w == chans - (CP - 8) + 1)

    def col_sum(v):
        return jnp.sum(v, axis=0, keepdims=True)

    def front(r, u):
        total = jnp.zeros((8, width), f32)
        for c in range(0, CP, 8):
            acc = None
            for tap in range(9):
                term = wide(kern_ref[tap, c : c + 8, :]) * field[r + tap // 3, tap % 3, c : c + 8, :]
                acc = term if acc is None else acc + term
            depth_s[u, c : c + 8, :] = acc
            total = total + acc
        mean = col_sum(total) * (1.0 / chans)
        square = jnp.zeros((8, width), f32)
        for c in range(0, CP, 8):
            d = depth_s[u, c : c + 8, :] - mean
            if c == CP - 8:
                d = d * tail
            depth_s[u, c : c + 8, :] = d
            square = square + d * d
        inv_std = lax.rsqrt(col_sum(square) * (1.0 / chans) + NORM_EPS)
        for c in range(0, CP, 16):
            parts = []
            for e in (c, c + 8):
                s = depth_s[u, e : e + 8, :] * inv_std
                scaled_s[u, e : e + 8, :] = s
                n = s * wide(vec_ref[1, e : e + 8, :]) + wide(vec_ref[2, e : e + 8, :])
                if e == CP - 8:
                    n = jnp.where(ones_rows, 1.0, n)
                parts.append(n)
            norm_s[u, c : c + 16, :] = jnp.concatenate(parts, axis=0).astype(bf16)
        cot = jnp.concatenate([cot_s[k, pl.ds(r, CP, stride=rows), :] for k in range(lanes)], axis=1)
        cotb_s[u] = cot.astype(bf16)
        pre_s[u] = jnp.dot(w1t_ref[...], norm_s[u], preferred_element_type=f32)
        back_s[u] = jnp.dot(w2_ref[...], cotb_s[u], preferred_element_type=f32)
        return inv_std

    def middle(u):
        for h in range(0, HP, 16):
            x = pre_s[u, h : h + 16, :]
            q = x * x
            t = jnp.tanh(x * (GELU_K + (GELU_K * GELU_C) * q))
            s = 0.5 + 0.5 * t
            g = x * s
            slope = s + (g - g * s) * (2.0 * GELU_K + (6.0 * GELU_K * GELU_C) * q)
            hid_s[u, h : h + 16, :] = g.astype(bf16)
            bp_s[u, h : h + 16, :] = (back_s[u, h : h + 16, :] * slope).astype(bf16)

    def rear(r, u, inv_std):
        out = jnp.dot(w2t_ref[...], hid_s[u], preferred_element_type=f32)
        out = out + wide(vec_ref[3]) + field[r + 1, 1]
        for k in range(lanes):
            out_s[k, pl.ds(r, CP, stride=rows), :] = out[:, k * 128 : (k + 1) * 128]
        bd_s[u] = jnp.dot(w1_ref[...], bp_s[u], preferred_element_type=f32)
        one = jnp.zeros((8, width), f32)
        two = jnp.zeros((8, width), f32)
        for c in range(0, CP, 8):
            b = bd_s[u, c : c + 8, :] * wide(vec_ref[1, c : c + 8, :])
            bd_s[u, c : c + 8, :] = b
            one = one + b
            two = two + b * scaled_s[u, c : c + 8, :]
        one = col_sum(one) * (inv_std * (1.0 / chans))
        two = col_sum(two) * (inv_std * (1.0 / chans))
        for c in range(0, CP, 8):
            b = bd_s[u, c : c + 8, :] * inv_std - one - scaled_s[u, c : c + 8, :] * two
            for tap in range(9):
                m = b * field[r + tap // 3, tap % 3, c : c + 8, :]
                m = sum(m[:, k * 128 : (k + 1) * 128] for k in range(lanes))
                gk_s[tap, c : c + 8, :] += m

    def step(i, _):
        stds = []
        for u in range(UNROLL):
            r = i * UNROLL + u
            nxt = jnp.minimum(r + 1, rows - 1)
            make_row(nxt + 1, row_of(nxt))
        for u in range(UNROLL):
            stds.append(front(i * UNROLL + u, u))
        for u in range(UNROLL):
            middle(u)
        for u in range(UNROLL):
            rear(i * UNROLL + u, u, stds[u])
        nt = (((1,), (1,)), ((), ()))
        g2_s[...] += sum(lax.dot_general(hid_s[u], cotb_s[u], nt, preferred_element_type=f32) for u in range(UNROLL))
        g1_s[...] += sum(lax.dot_general(bp_s[u], norm_s[u], nt, preferred_element_type=f32) for u in range(UNROLL))
        return 0

    lax.fori_loop(0, rows // UNROLL, step, 0)

    def back(c, _):
        x = jnp.concatenate(
            [out_s[k, pl.ds(pl.multiple_of(c * rows, rows), rows), :] for k in range(lanes)], axis=1
        )
        out_ref[c] = x.astype(bf16)
        return 0

    lax.fori_loop(0, chans, back, 0)
    grad_ref[...] = jnp.zeros_like(grad_ref)
    grad_ref[0:360, 0:CP] = g2_s[0:360, :] * scale
    grad_ref[360:720, 0:CP] = g1_s[0:360, :] * scale
    ones = jnp.ones((8, 128), f32)
    for tap in range(9):
        line = lax.dot_general(
            ones, gk_s[tap], (((1,), (1,)), ((), ())), preferred_element_type=f32, precision=lax.Precision.HIGHEST
        )
        grad_ref[720 + tap : 721 + tap, 0:CP] = line[0:1, :] * scale


def strip_call(inv, flags, blocks, rows, cols, cot, w_in, b_in, kernel, ln_gain, ln_bias, w_one, b_one, w_two, b_two, scale):
    chans, nrow, width = cot.shape
    pad_c = CP - chans
    pad_h = HP - w_one.shape[1]
    win = jnp.pad(w_in.T, ((0, pad_c), (0, 0)))
    table = jnp.pad(jnp.concatenate([jnp.stack([b_in, ln_gain, ln_bias, b_two]), kernel]), ((0, 0), (0, pad_c)))
    table = jnp.broadcast_to(table[:, :, None], (13, CP, 128))
    vec, kern = table[:4], table[4:]
    high = b_one.astype(jnp.bfloat16)
    low = (b_one - high.astype(jnp.float32)).astype(jnp.bfloat16)
    w1t = jnp.pad(jnp.concatenate([w_one, high[None], low[None]]).T, ((0, pad_h), (0, pad_c - 2)))
    w2t = jnp.pad(w_two.T, ((0, pad_c), (0, pad_h)))
    w1 = jnp.pad(w_one, ((0, pad_c), (0, pad_h)))
    w2 = jnp.pad(w_two, ((0, pad_h), (0, pad_c)))
    f32, bf16 = jnp.float32, jnp.bfloat16
    lanes = width // 128
    vm = pl.BlockSpec(memory_space=pltpu.VMEM)
    sm = pl.BlockSpec(memory_space=pltpu.SMEM)
    return pl.pallas_call(
        functools.partial(strip_kernel, scale=scale),
        out_shape=(jax.ShapeDtypeStruct((chans, nrow, width), bf16), jax.ShapeDtypeStruct((768, 128), f32)),
        in_specs=[sm, sm] + [vm] * 11,
        out_specs=(vm, vm),
        scratch_shapes=[
            pltpu.VMEM((nrow + 2, 3, CP, width), f32),
            pltpu.VMEM((2, CP, 128), f32),
            pltpu.VMEM((lanes, CP * nrow, 128), f32),
            pltpu.VMEM((lanes, CP * nrow, 128), f32),
            pltpu.VMEM((UNROLL, CP, width), f32),
            pltpu.VMEM((UNROLL, CP, width), f32),
            pltpu.VMEM((UNROLL, CP, width), bf16),
            pltpu.VMEM((UNROLL, CP, width), bf16),
            pltpu.VMEM((UNROLL, HP, width), f32),
            pltpu.VMEM((UNROLL, HP, width), f32),
            pltpu.VMEM((UNROLL, HP, width), bf16),
            pltpu.VMEM((UNROLL, HP, width), bf16),
            pltpu.VMEM((UNROLL, CP, width), f32),
            pltpu.VMEM((HP, CP), f32),
            pltpu.VMEM((HP, CP), f32),
            pltpu.VMEM((9, CP, 128), f32),
        ],
        compiler_params=pltpu.CompilerParams(vmem_limit_bytes=58 * MIB),
    )(inv, flags, blocks, rows, cols, cot, win, vec, kern, w1t, w2t, w1, w2)


MESH = pl.DeviceIdType.MESH
MIB = 1024 * 1024
VM = pl.BlockSpec(memory_space=pltpu.VMEM)
SM = pl.BlockSpec(memory_space=pltpu.SMEM)
AXES = ("face", "tile")


def partial_kernel(pick_ref, slot_ref, source_ref, weight_ref, out_ref, part):
    count = weight_ref.shape[0]
    group = 8

    def one(i, _):
        for k in range(group):
            e = i * group + k
            x = jnp.dot(source_ref[pick_ref[e]], weight_ref[e], preferred_element_type=jnp.float32)
            part[e] = x.astype(jnp.bfloat16)
        return 0

    lax.fori_loop(0, count // group, one, 0)

    def put(d, _):
        out_ref[d, 0:16, :] = part[slot_ref[2 * d]]
        out_ref[d, 16:32, :] = part[slot_ref[2 * d + 1]]
        return 0

    lax.fori_loop(0, count, put, 0, unroll=8)


def partial_call(pick, slots, source, weight):
    count = weight.shape[0]
    return pl.pallas_call(
        partial_kernel,
        out_shape=jax.ShapeDtypeStruct((count, 32, 128), jnp.bfloat16),
        in_specs=[SM, SM, VM, VM],
        out_specs=VM,
        scratch_shapes=[pltpu.VMEM((count, 16, 128), jnp.bfloat16)],
        compiler_params=pltpu.CompilerParams(vmem_limit_bytes=32 * MIB),
    )(pick, slots, source, weight)


def exchange_kernel(faces, tiles, index, *refs):
    if index:
        ids_ref, box_ref, all_ref, got_ref, send, recv, local, send_a, recv_a, send_b, recv_b = refs
    else:
        box_ref, got_ref, send, recv, local = refs
    face = lax.axis_index("face")
    tile = lax.axis_index("tile")
    count = faces * tiles
    me = face * tiles + tile
    barrier = pltpu.get_barrier_semaphore()

    def greet(k, _):
        peer = lax.rem(me + k, count)
        pl.semaphore_signal(barrier, inc=1, device_id=(peer // tiles, lax.rem(peer, tiles)), device_id_type=MESH)
        return 0

    lax.fori_loop(1, count, greet, 0)
    pl.semaphore_wait(barrier, count - 1)

    if index:
        all_ref[face, tile] = ids_ref[...]
        first = []
        for k in range(1, tiles):
            first.append(
                pltpu.make_async_remote_copy(
                    src_ref=ids_ref,
                    dst_ref=all_ref.at[face, tile],
                    send_sem=send_a.at[k],
                    recv_sem=recv_a.at[k],
                    device_id=(face, lax.rem(tile + k, tiles)),
                    device_id_type=MESH,
                )
            )
            first[-1].start()

    def push(k, _):
        peer = lax.rem(me + k, count)
        pltpu.make_async_remote_copy(
            src_ref=box_ref.at[peer],
            dst_ref=got_ref.at[me],
            send_sem=send,
            recv_sem=recv,
            device_id=(peer // tiles, lax.rem(peer, tiles)),
            device_id_type=MESH,
        ).start()
        return 0

    lax.fori_loop(1, count, push, 0)
    own = pltpu.make_async_copy(box_ref.at[me], got_ref.at[me], local)
    own.start()
    if index:
        for copy in first:
            copy.wait()
        second = []
        for k in range(1, faces):
            second.append(
                pltpu.make_async_remote_copy(
                    src_ref=all_ref.at[face],
                    dst_ref=all_ref.at[face],
                    send_sem=send_b.at[k],
                    recv_sem=recv_b.at[k],
                    device_id=(lax.rem(face + k, faces), tile),
                    device_id_type=MESH,
                )
            )
            second[-1].start()
        for copy in second:
            copy.wait()
    own.wait()
    whole = pl.ds(0, count - 1)
    pltpu.make_async_copy(box_ref.at[whole], got_ref.at[whole], send).wait()
    pltpu.make_async_copy(box_ref.at[whole], got_ref.at[whole], recv).wait()


def exchange_call(box, ids, collective_id):
    faces, tiles = lax.axis_size("face"), lax.axis_size("tile")
    index = ids is not None
    out = [jax.ShapeDtypeStruct(box.shape, box.dtype)]
    args = [box]
    dma = pltpu.SemaphoreType.DMA
    scratch = [dma, dma, dma]
    if index:
        out = [jax.ShapeDtypeStruct((faces, tiles) + ids.shape, ids.dtype)] + out
        args = [ids] + args
        scratch += [dma((tiles,)), dma((tiles,)), dma((faces,)), dma((faces,))]
    return pl.pallas_call(
        functools.partial(exchange_kernel, faces, tiles, index),
        out_shape=tuple(out),
        in_specs=[VM] * len(args),
        out_specs=tuple([VM] * len(out)),
        scratch_shapes=scratch,
        compiler_params=pltpu.CompilerParams(
            collective_id=collective_id, has_side_effects=True, vmem_limit_bytes=32 * MIB
        ),
    )(*args)


def combine_kernel(label_ref, perm_ref, got_ref, out_ref, total):
    count = got_ref.shape[0]
    total[...] = jnp.zeros_like(total)

    def add(s, _):
        for k in range(2):
            spot = label_ref[2 * s + k]
            total[spot] += got_ref[s, 16 * k : 16 * k + 16, :].astype(jnp.float32)
        return 0

    lax.fori_loop(0, count, add, 0)

    def put(d, _):
        out_ref[d] = total[perm_ref[d]].astype(jnp.bfloat16)
        return 0

    lax.fori_loop(0, count, put, 0, unroll=8)


def combine_call(labels, perm, got):
    count = got.shape[0]
    return pl.pallas_call(
        combine_kernel,
        out_shape=jax.ShapeDtypeStruct((count, 16, 128), jnp.bfloat16),
        in_specs=[SM, SM, VM],
        out_specs=VM,
        scratch_shapes=[pltpu.VMEM((count + 1, 16, 128), jnp.float32)],
        compiler_params=pltpu.CompilerParams(vmem_limit_bytes=32 * MIB),
    )(labels, perm, got)


def lines_kernel(
    faces, tiles, inv_ref, link_ref, box_ref, rows_ref, cols_ref, edge, upper, lower, packet, packets, ends, line, wins,
    lots, windows, whole, send_v, recv_v, send_p, recv_p, send_e, recv_e, send_w, recv_w, send_l, recv_l,
):
    f32, bf16 = jnp.float32, jnp.bfloat16
    face = lax.axis_index("face")
    tile = lax.axis_index("tile")
    chans = box_ref.shape[1]
    nrow = box_ref.shape[0] // 4
    barrier = pltpu.get_barrier_semaphore()
    for k in range(1, tiles):
        pl.semaphore_signal(barrier, inc=1, device_id=(face, lax.rem(tile + k, tiles)), device_id_type=MESH)
    for k in range(1, faces):
        pl.semaphore_signal(barrier, inc=1, device_id=(lax.rem(face + k, faces), tile), device_id_type=MESH)
    pl.semaphore_wait(barrier, tiles + faces - 2)

    for k in range(4):
        edge[0, k] = box_ref[inv_ref[k]]
        edge[1, k] = box_ref[inv_ref[4 * nrow - 4 + k]]
    down = lax.rem(tile + 1, tiles)
    up = lax.rem(tile + tiles - 1, tiles)
    vertical = []
    for k, (dst, peer) in enumerate(((upper, down), (lower, up))):
        vertical.append(
            pltpu.make_async_remote_copy(
                src_ref=edge.at[1 - k],
                dst_ref=dst,
                send_sem=send_v.at[k],
                recv_sem=recv_v.at[k],
                device_id=(face, peer),
                device_id_type=MESH,
            )
        )
        vertical[-1].start()

    def end_copy(k, side):
        return pltpu.make_async_remote_copy(
            src_ref=edge.at[side],
            dst_ref=ends.at[side],
            send_sem=send_e.at[k],
            recv_sem=recv_e.at[side],
            device_id=(face, lax.rem(tile + k, tiles)),
            device_id_type=MESH,
        )

    for side, owner in ((0, 0), (1, tiles - 1)):

        @pl.when(tile == owner)
        def _():
            for k in range(1, tiles):
                end_copy(k, side).start()
            ends[side] = edge[side]

    lane = lax.broadcasted_iota(jnp.int32, (chans, 128), 1)

    def pick(r, acc):
        left = pltpu.roll(box_ref[inv_ref[4 * r]].astype(f32), r, 1)
        right = pltpu.roll(box_ref[inv_ref[4 * r + 3]].astype(f32), r + nrow + 1, 1)
        return jnp.where(lane == r, left, jnp.where(lane == r + nrow, right, acc))

    packet[...] = lax.fori_loop(0, nrow, pick, jnp.zeros((chans, 128), f32), unroll=8).astype(bf16)
    packets[tile] = packet[...]
    sends = []
    for k in range(1, tiles):
        sends.append(
            pltpu.make_async_remote_copy(
                src_ref=packet,
                dst_ref=packets.at[tile],
                send_sem=send_p.at[k],
                recv_sem=recv_p.at[k],
                device_id=(face, lax.rem(tile + k, tiles)),
                device_id_type=MESH,
            )
        )
        sends[-1].start()
    for copy in sends:
        copy.wait()
    for side, owner in ((0, 0), (1, tiles - 1)):

        @pl.when(tile == owner)
        def _():
            for k in range(1, tiles):
                end_copy(k, side).wait_send()

        @pl.when(tile != owner)
        def _():
            end_copy(1, side).wait_recv()

    per = 128 // nrow
    for side in range(2):
        line[side] = jnp.concatenate([ends[side, k] for k in range(4)], axis=1).astype(f32)
        parts = []
        for block in range(tiles // per):
            acc = jnp.zeros((chans, 128), f32)
            for i in range(per):
                seg = packets[block * per + i].astype(f32)
                seg = pltpu.roll(seg, (128 + (i - side) * nrow) % 128, 1) if i != side else seg
                acc = jnp.where((lane >= i * nrow) & (lane < (i + 1) * nrow), seg, acc)
            parts.append(acc)
        line[2 + side] = jnp.concatenate(parts, axis=1)
    width = tiles * nrow
    for s in range(4):
        full = line[s]
        for k in range(4):
            lots[s, k] = full[:, k * 128 : (k + 1) * 128].astype(bf16)
        near = pltpu.roll(full, lax.rem(width + 1 - tile * nrow, width), 1)[:, 0:128]
        far = pltpu.roll(full, lax.rem(width + 65 - (tiles - 1 - tile) * nrow, width), 1)[:, 0:128]
        wins[s] = jnp.where(lane < 64, near, far).astype(bf16)
    windows[face] = wins[...]
    sends = []
    for k in range(1, faces):
        sends.append(
            pltpu.make_async_remote_copy(
                src_ref=wins,
                dst_ref=windows.at[face],
                send_sem=send_w.at[k],
                recv_sem=recv_w.at[k],
                device_id=(lax.rem(face + k, faces), tile),
                device_id_type=MESH,
            )
        )
        sends[-1].start()

    def lot_copy(k):
        return pltpu.make_async_remote_copy(
            src_ref=lots,
            dst_ref=whole.at[face],
            send_sem=send_l.at[k],
            recv_sem=recv_l.at[k],
            device_id=(lax.rem(face + k, faces), tile),
            device_id_type=MESH,
        )

    at_end = (tile == 0) | (tile == tiles - 1)

    @pl.when(at_end)
    def _():
        for k in range(1, faces):
            lot_copy(k).start()
        whole[face] = lots[...]

    for copy in vertical:
        copy.wait()
    for copy in sends:
        copy.wait()
    row = lax.broadcasted_iota(jnp.int32, (128, 128), 0)
    col = lax.broadcasted_iota(jnp.int32, (128, 128), 1)
    at = 4 * (face * 3)
    for side in range(2):
        base = (face * 4 + 2 + side) * 3
        view = windows[link_ref[base], link_ref[base + 1]]
        spot = jnp.where(link_ref[base + 2] == 1, 65 + nrow - col, col)
        turn = (row == spot).astype(bf16)
        cols_ref[side] = jnp.dot(view, turn, preferred_element_type=f32).astype(bf16)
        rows_ref[side] = (upper, lower)[side][...]

    @pl.when(at_end)
    def _():
        for k in range(1, faces):
            lot_copy(k).wait()

    for side, owner in ((0, 0), (1, tiles - 1)):

        @pl.when(tile == owner)
        def _():
            base = (face * 4 + side) * 3
            flip = link_ref[base + 2] == 1
            turn = (row == jnp.where(flip, 127 - col, col)).astype(bf16)
            for k in range(4):
                view = whole[link_ref[base], link_ref[base + 1], jnp.where(flip, 3 - k, k)]
                rows_ref[side, k] = jnp.dot(view, turn, preferred_element_type=f32).astype(bf16)


def lines_call(inv, links, box, collective_id):
    faces, tiles = lax.axis_size("face"), lax.axis_size("tile")
    dma = pltpu.SemaphoreType.DMA
    bf16 = jnp.bfloat16
    chans = box.shape[1]
    block = (4, chans, 128)
    return pl.pallas_call(
        functools.partial(lines_kernel, faces, tiles),
        out_shape=(jax.ShapeDtypeStruct((2,) + block, bf16), jax.ShapeDtypeStruct((2, chans, 128), bf16)),
        in_specs=[SM, SM, VM],
        out_specs=(VM, VM),
        scratch_shapes=[
            pltpu.VMEM((2,) + block, bf16),
            pltpu.VMEM(block, bf16),
            pltpu.VMEM(block, bf16),
            pltpu.VMEM((chans, 128), bf16),
            pltpu.VMEM((tiles, chans, 128), bf16),
            pltpu.VMEM((2,) + block, bf16),
            pltpu.VMEM((4, chans, 512), jnp.float32),
            pltpu.VMEM(block, bf16),
            pltpu.VMEM((4,) + block, bf16),
            pltpu.VMEM((faces,) + block, bf16),
            pltpu.VMEM((faces, 4) + block, bf16),
            dma((2,)), dma((2,)), dma((tiles,)), dma((tiles,)), dma((tiles,)), dma((2,)), dma((faces,)), dma((faces,)),
            dma((faces,)), dma((faces,)),
        ],
        compiler_params=pltpu.CompilerParams(
            collective_id=collective_id, has_side_effects=True, vmem_limit_bytes=32 * MIB
        ),
    )(inv, links, box)


def reduce_kernel(
    faces, tiles, grad_ref, one_ref, two_ref, ker_ref, first, part, second, mine, full, send_a, recv_a, send_b, recv_b,
    send_c, recv_c,
):
    face = lax.axis_index("face")
    tile = lax.axis_index("tile")
    size = grad_ref.shape[0] // tiles
    barrier = pltpu.get_barrier_semaphore()
    for k in range(1, tiles):
        pl.semaphore_signal(barrier, inc=1, device_id=(face, lax.rem(tile + k, tiles)), device_id_type=MESH)
    for k in range(1, faces):
        pl.semaphore_signal(barrier, inc=1, device_id=(lax.rem(face + k, faces), tile), device_id_type=MESH)
    pl.semaphore_wait(barrier, tiles + faces - 2)

    def spot(t):
        return pl.ds(pl.multiple_of(t * size, 8), size)

    copies = []
    for k in range(1, tiles):
        peer = lax.rem(tile + k, tiles)
        copies.append(
            pltpu.make_async_remote_copy(
                src_ref=grad_ref.at[spot(peer)],
                dst_ref=first.at[k],
                send_sem=send_a.at[k],
                recv_sem=recv_a.at[k],
                device_id=(face, peer),
                device_id_type=MESH,
            )
        )
        copies[-1].start()
    total = grad_ref[spot(tile), :]
    for k in range(1, tiles):
        copies[k - 1].wait_recv()
        total = total + first[k]
    part[...] = total
    second[face] = total
    later = []
    for k in range(1, faces):
        later.append(
            pltpu.make_async_remote_copy(
                src_ref=part,
                dst_ref=second.at[face],
                send_sem=send_b.at[k],
                recv_sem=recv_b.at[k],
                device_id=(lax.rem(face + k, faces), tile),
                device_id_type=MESH,
            )
        )
        later[-1].start()
    for copy in later:
        copy.wait_recv()
    total = second[0]
    for k in range(1, faces):
        total = total + second[k]
    mine[...] = total
    full[spot(tile), :] = total
    last = []
    for k in range(1, tiles):
        last.append(
            pltpu.make_async_remote_copy(
                src_ref=mine,
                dst_ref=full.at[spot(tile)],
                send_sem=send_c.at[k],
                recv_sem=recv_c.at[k],
                device_id=(face, lax.rem(tile + k, tiles)),
                device_id_type=MESH,
            )
        )
        last[-1].start()
    for copy in last:
        copy.wait_recv()
    two_ref[...] = full[0:360, 0:90]
    one_ref[...] = full[360:720, 0:128].T[0:90, :]
    ker_ref[...] = full[720:729, 0:90]
    for copy in copies + later + last:
        copy.wait_send()


def reduce_call(grad, collective_id):
    faces, tiles = lax.axis_size("face"), lax.axis_size("tile")
    dma = pltpu.SemaphoreType.DMA
    f32 = jnp.float32
    size = grad.shape[0] // tiles
    return pl.pallas_call(
        functools.partial(reduce_kernel, faces, tiles),
        out_shape=(
            jax.ShapeDtypeStruct((90, 360), f32),
            jax.ShapeDtypeStruct((360, 90), f32),
            jax.ShapeDtypeStruct((9, 90), f32),
        ),
        in_specs=[VM],
        out_specs=(VM, VM, VM),
        scratch_shapes=[
            pltpu.VMEM((tiles, size, 128), f32),
            pltpu.VMEM((size, 128), f32),
            pltpu.VMEM((faces, size, 128), f32),
            pltpu.VMEM((size, 128), f32),
            pltpu.VMEM(grad.shape, f32),
            dma((tiles,)), dma((tiles,)), dma((faces,)), dma((faces,)), dma((tiles,)), dma((tiles,)),
        ],
        compiler_params=pltpu.CompilerParams(
            collective_id=collective_id, has_side_effects=True, vmem_limit_bytes=32 * MIB
        ),
    )(grad)


def remap(source, entry_block, entry_source, entry_weight, lat_to_nested):
    count = entry_block.shape[0]
    me = lax.axis_index("face") * lax.axis_size("tile") + lax.axis_index("tile")
    ids = jnp.arange(count, dtype=jnp.int32)
    owner = entry_block // count
    hit = owner[None, :] == ids[:, None]
    low = jnp.min(jnp.where(hit, ids[None, :], count - 1), axis=1)
    high = jnp.max(jnp.where(hit, ids[None, :], 0), axis=1)
    slots = jnp.stack([low, high], axis=1).reshape(-1)
    perm = jnp.sum(jnp.where((lat_to_nested // count)[None, :] == ids[:, None], ids[None, :], 0), axis=1)
    box = partial_call(entry_source, slots, source, entry_weight)
    table, got = exchange_call(box, jnp.stack([entry_block, lat_to_nested]), 1)
    table = table.reshape(count, 2, count)
    key = ids[None, :] * count + table[:, 0] % count
    hit = table[:, 0] // count == me
    low = jnp.min(jnp.where(hit, key, count * count), axis=1)
    high = jnp.max(jnp.where(hit, key, -1), axis=1)
    label_low = jnp.where(high >= 0, low % count, count)
    label_high = jnp.where(high > low, high % count, count)
    labels = jnp.stack([label_low, label_high], axis=1).reshape(-1)
    spots = jnp.sum(jnp.where(table[:, 1] // count == me, table[:, 1] % count, 0), axis=1)
    inv = jnp.sum(jnp.where(spots[None, :] == ids[:, None], ids[None, :], 0), axis=1)
    out = combine_call(labels, perm, got)
    return inv, exchange_call(out, None, 2)[0]

def per_device(
    source, entry_block, entry_source, entry_weight, lat_to_nested, face_links, w_in, b_in, kernel, ln_gain, ln_bias,
    w_one, b_one, w_two, b_two, cotangent,
):
    tile_at = lax.axis_index("tile")
    face_count, tile_count = lax.axis_size("face"), lax.axis_size("tile")
    width = cotangent.shape[3]
    inv, box = remap(source, entry_block, entry_source, entry_weight, lat_to_nested)
    rows, cols = lines_call(inv, face_links.reshape(-1), box, 3)
    flags = jnp.stack([tile_at == 0, tile_at == tile_count - 1]).astype(jnp.int32)
    scale = 1.0 / math.sqrt(face_count * width * width)
    output, grad = strip_call(
        inv, flags, box, rows, cols, cotangent[0], w_in, b_in, kernel, ln_gain, ln_bias, w_one, b_one, w_two, b_two,
        scale,
    )
    grad_one, grad_two, grad_kernel = reduce_call(grad, 4)
    return (output[None], grad_one, grad_two, grad_kernel)


def solution(mesh):
    split = P(("face", "tile"))
    strips = P("face", None, "tile", None)
    return jax.shard_map(
        per_device,
        mesh=mesh,
        in_specs=(split,) * 5 + (P(),) * 10 + (strips,),
        out_specs=(strips, P(), P(), P()),
        check_vma=False,
    )
```

```python
import functools
import math

import jax
import jax.numpy as jnp
from jax import lax
from jax.experimental import pallas as pl
from jax.experimental.pallas import tpu as pltpu
from jax.sharding import PartitionSpec as P


GELU_K = 0.7978845608028654
GELU_C = 0.044715
NORM_EPS = 1e-06
CP = 96
HP = 368
PITCH = 40
UNROLL = 2
HID = 16
MIB = 1024 * 1024


def strip_kernel(
    inv_ref, flag_ref, blocks_ref, rows_ref, cols_ref, cot_ref, win_ref, bin_ref, ker_ref, gain_ref, bias_ref, wone_ref,
    bone_ref, wtwo_ref, btwo_ref, out_ref, grad_ref, field, cols, depth, cot_s, out_s, scaled_s, norm_s, cotb_s,
    pre_s, back_s, hid_s, bp_s, g2_s, g1_s, gk_s, tab_s, vec_s, flat_s, tall_s, w_in_s, w1t_s, w1_s, w2t_s, w2_s, scale,
):
    chans, rows, width = cot_ref.shape
    hidden = wone_ref.shape[1]
    lanes = width // 128
    f32, bf16 = jnp.float32, jnp.bfloat16
    nt = (((1,), (1,)), ((), ()))

    def wide(v):
        return jnp.concatenate([v] * lanes, axis=1)

    tab_s[...] = jnp.zeros_like(tab_s)
    for j, ref in enumerate((bin_ref, gain_ref, bias_ref, btwo_ref)):
        tab_s[j : j + 1, 0:chans] = ref[...]
    tab_s[4:13, 0:chans] = ker_ref[...]
    turned = tab_s[...].T
    for j in range(13):
        vec_s[j] = jnp.broadcast_to(turned[0:CP, j : j + 1], (CP, 128))
    tab_s[...] = jnp.zeros_like(tab_s)
    tab_s[0:16, 0:chans] = win_ref[...].astype(f32)
    w_in_s[...] = tab_s[...].T[0:CP, 0:16].astype(bf16)
    flat_s[...] = jnp.zeros_like(flat_s)
    flat_s[0:chans, 0:hidden] = wone_ref[...].astype(f32)
    w1_s[...] = flat_s[0:CP, 0:HP].astype(bf16)
    high = bone_ref[...].astype(bf16).astype(f32)
    flat_s[chans : chans + 1, 0:hidden] = high
    flat_s[chans + 1 : chans + 2, 0:hidden] = bone_ref[...] - high
    w1t_s[...] = (flat_s[...].T[0:HP, 0:CP] * 0.5).astype(bf16)
    tall_s[...] = jnp.zeros_like(tall_s)
    tall_s[0:hidden, 0:chans] = wtwo_ref[...].astype(f32)
    w2_s[...] = (tall_s[0:HP, 0:CP] * 0.5).astype(bf16)
    w2t_s[...] = tall_s[...].T[0:CP, 0:HP].astype(bf16)

    lane = lax.broadcasted_iota(jnp.int32, (CP, 128), 1)
    last = lane == jnp.where(flag_ref[1] == 1, rows + 1, -1)
    first = lane == jnp.where(flag_ref[0] == 1, 0, -1)
    for side in range(2):
        v = jnp.dot(w_in_s[...], cols_ref[side], preferred_element_type=f32) + vec_s[0]
        cols[side] = jnp.where(first | last, 0.0, v.astype(bf16).astype(f32))

    g2_s[...] = jnp.zeros_like(g2_s)
    g1_s[...] = jnp.zeros_like(g1_s)
    cot_s[:, chans * PITCH :, :] = jnp.zeros((lanes, (CP - chans) * PITCH, 128), f32)

    def turn(c, _):
        x = cot_ref[c].astype(f32)
        for k in range(lanes):
            cot_s[k, pl.ds(pl.multiple_of(c * PITCH, 8), rows), :] = x[:, k * 128 : (k + 1) * 128]
        return 0

    lax.fori_loop(0, chans, turn, 0, unroll=2)

    def make_row(at, x):
        lat = jnp.dot(w_in_s[...], x, preferred_element_type=f32) + wide(vec_s[0])
        lat = lat.astype(bf16).astype(f32)
        wide_lane = lax.broadcasted_iota(jnp.int32, (CP, 128), 1)
        mid = [lat[:, k * 128 : (k + 1) * 128] for k in range(lanes)]
        up = [pltpu.roll(cols[0], lax.rem(128 - at, 128), 1)] + [pltpu.roll(m, 1, 1) for m in mid]
        dn = [pltpu.roll(m, 127, 1) for m in mid] + [pltpu.roll(cols[1], 127 - at, 1)]
        for k in range(lanes):
            part = slice(k * 128, (k + 1) * 128)
            field[at, 0, :, part] = jnp.where(wide_lane == 0, up[k], up[k + 1])
            field[at, 1, :, part] = mid[k]
            field[at, 2, :, part] = jnp.where(wide_lane == 127, dn[k + 1], dn[k])

    make_row(0, jnp.concatenate([rows_ref[0, k] for k in range(lanes)], axis=1))
    make_row(rows + 1, jnp.concatenate([rows_ref[1, k] for k in range(lanes)], axis=1))

    def row_step(r, _):
        make_row(r + 1, jnp.concatenate([blocks_ref[inv_ref[r * lanes + k]] for k in range(lanes)], axis=1))
        return 0

    lax.fori_loop(0, rows, row_step, 0, unroll=2)

    def shifted(r, c):
        return [
            [field[r, side, pl.ds(c, 8), k * 128 : (k + 1) * 128] for k in range(lanes)] for side in range(3)
        ]

    def conv_chunk(i, _):
        c = pl.multiple_of(i * 8, 8)
        w = [vec_s[4 + tap, pl.ds(c, 8), :] for tap in range(9)]

        def mix(a, views, k):
            return w[3 * a] * views[0][k] + w[3 * a + 1] * views[1][k] + w[3 * a + 2] * views[2][k]

        v0, v1 = shifted(0, c), shifted(1, c)
        one = tuple(mix(0, v0, k) + mix(1, v1, k) for k in range(lanes))
        two = tuple(mix(0, v1, k) for k in range(lanes))

        def go(r, carry):
            one, two = carry
            v = shifted(r + 2, c)
            for k in range(lanes):
                depth[r, pl.ds(c, 8), k * 128 : (k + 1) * 128] = one[k] + mix(2, v, k)
            return (
                tuple(two[k] + mix(1, v, k) for k in range(lanes)),
                tuple(mix(0, v, k) for k in range(lanes)),
            )

        lax.fori_loop(0, rows, go, (one, two), unroll=4)
        return 0

    lax.fori_loop(0, CP // 8, conv_chunk, 0)

    row_id = lax.broadcasted_iota(jnp.int32, (CP, 128), 0)
    real = row_id < chans
    ones_rows = (row_id == chans) | (row_id == chans + 1)

    def col_sum(v):
        return jnp.sum(v, axis=0, keepdims=True)

    def front(r, u):
        stds = []
        for k in range(lanes):
            part = slice(k * 128, (k + 1) * 128)
            d = depth[r, :, part]
            d = d - col_sum(d) * (1.0 / chans)
            d = jnp.where(real, d, 0.0)
            inv_std = lax.rsqrt(col_sum(d * d) * (1.0 / chans) + NORM_EPS)
            s = d * inv_std
            scaled_s[u, :, part] = s
            n = jnp.where(ones_rows, 1.0, s * vec_s[1] + vec_s[2])
            norm_s[u, :, part] = n.astype(bf16)
            cotb_s[u, :, part] = cot_s[k, pl.ds(r, CP, stride=PITCH), :].astype(bf16)
            stds.append(inv_std)
        pre_s[u] = jnp.dot(w1t_s[...], norm_s[u], preferred_element_type=f32).astype(pre_s.dtype)
        back_s[u] = jnp.dot(w2_s[...], cotb_s[u], preferred_element_type=f32).astype(back_s.dtype)
        return stds

    def middle(u):
        ty = pre_s.dtype
        num = lambda v: jnp.asarray(v, ty)
        for h in range(0, HP, 16):
            x = pre_s[u, h : h + 16, :]
            q = x * x
            t = jnp.tanh(x * (num(2.0 * GELU_K) + num(8.0 * GELU_K * GELU_C) * q))
            p = num(1.0) + t
            g = x * p
            slope = p + g * (num(1.0) - t) * (num(2.0 * GELU_K) + num(24.0 * GELU_K * GELU_C) * q)
            hid_s[u, h : h + 16, :] = g.astype(bf16)
            bp_s[u, h : h + 16, :] = (back_s[u, h : h + 16, :] * slope).astype(bf16)

    def rear(r, u, stds):
        out = jnp.dot(w2t_s[...], hid_s[u], preferred_element_type=f32)
        hat = jnp.dot(w1_s[...], bp_s[u], preferred_element_type=f32)
        for k in range(lanes):
            part = slice(k * 128, (k + 1) * 128)
            out_s[k, pl.ds(r, CP, stride=PITCH), :] = out[:, part] + vec_s[3] + field[r + 1, 1, :, part]
            b = hat[:, part] * vec_s[1]
            s = scaled_s[u, :, part]
            one = col_sum(b) * (stds[k] * (1.0 / chans))
            two = col_sum(b * s) * (stds[k] * (1.0 / chans))
            depth[r, :, part] = b * stds[k] - one - s * two

    def step(i, _):
        stds = [front(i * UNROLL + u, u) for u in range(UNROLL)]
        for u in range(UNROLL):
            middle(u)
        for u in range(UNROLL):
            rear(i * UNROLL + u, u, stds[u])
        g2_s[...] += sum(lax.dot_general(hid_s[u], cotb_s[u], nt, preferred_element_type=f32) for u in range(UNROLL))
        g1_s[...] += sum(lax.dot_general(bp_s[u], norm_s[u], nt, preferred_element_type=f32) for u in range(UNROLL))
        return 0

    lax.fori_loop(0, rows // UNROLL, step, 0)

    def back(c, _):
        x = jnp.concatenate([out_s[k, pl.ds(pl.multiple_of(c * PITCH, 8), rows), :] for k in range(lanes)], axis=1)
        out_ref[c] = x.astype(bf16)
        return 0

    lax.fori_loop(0, chans, back, 0, unroll=2)

    def kernel_chunk(i, _):
        c = pl.multiple_of(i * 8, 8)

        def grad_row(r):
            return tuple(depth[r, pl.ds(c, 8), k * 128 : (k + 1) * 128] for k in range(lanes))

        def fold(acc, a, b, views):
            new = list(acc)
            for s in range(3):
                m = b[0] * views[s][0]
                for k in range(1, lanes):
                    m = m + b[k] * views[s][k]
                new[3 * a + s] = new[3 * a + s] + m
            return tuple(new)

        acc = tuple(jnp.zeros((8, 128), f32) for _ in range(9))
        b0 = grad_row(0)
        acc = fold(acc, 0, b0, shifted(0, c))
        b1 = grad_row(1)
        v = shifted(1, c)
        acc = fold(fold(acc, 0, b1, v), 1, b0, v)

        def go(r, carry):
            acc, b1, b0 = carry
            v = shifted(r, c)
            b = grad_row(r)
            acc = fold(fold(fold(acc, 0, b, v), 1, b1, v), 2, b0, v)
            return acc, b, b1

        acc, b1, b0 = lax.fori_loop(2, rows, go, (acc, b1, b0), unroll=3)
        v = shifted(rows, c)
        acc = fold(fold(acc, 1, b1, v), 2, b0, v)
        acc = fold(acc, 2, b1, shifted(rows + 1, c))
        for tap in range(9):
            gk_s[tap, pl.ds(c, 8), :] = acc[tap]
        return 0

    lax.fori_loop(0, CP // 8, kernel_chunk, 0)
    grad_ref[720:768, :] = jnp.zeros((48, 128), f32)
    grad_ref[0:hidden, 0:CP] = g2_s[0:hidden, :] * scale
    grad_ref[hidden : 2 * hidden, 0:CP] = g1_s[0:hidden, :] * scale
    ones = jnp.ones((8, 128), f32)
    for tap in range(9):
        line = lax.dot_general(ones, gk_s[tap], nt, preferred_element_type=f32, precision=lax.Precision.HIGHEST)
        grad_ref[720 + tap : 721 + tap, 0:CP] = line[0:1, :] * scale


def strip_call(inv, flags, blocks, rows, cols, cot, w_in, b_in, kernel, ln_gain, ln_bias, w_one, b_one, w_two, b_two, scale):
    chans, nrow, width = cot.shape
    f32, bf16 = jnp.float32, jnp.bfloat16
    lanes = width // 128
    act = bf16 if HID == 16 else f32
    vm = pl.BlockSpec(memory_space=pltpu.VMEM)
    sm = pl.BlockSpec(memory_space=pltpu.SMEM)
    mem = pltpu.VMEM
    return pl.pallas_call(
        functools.partial(strip_kernel, scale=scale),
        out_shape=(jax.ShapeDtypeStruct((chans, nrow, width), bf16), jax.ShapeDtypeStruct((768, 128), f32)),
        in_specs=[sm, sm] + [vm] * 13,
        out_specs=(vm, vm),
        scratch_shapes=[
            mem((nrow + 2, 3, CP, width), f32),
            mem((2, CP, 128), f32),
            mem((nrow, CP, width), f32),
            mem((lanes, CP * PITCH, 128), f32),
            mem((lanes, CP * PITCH, 128), f32),
            mem((UNROLL, CP, width), f32),
            mem((UNROLL, CP, width), bf16),
            mem((UNROLL, CP, width), bf16),
            mem((UNROLL, HP, width), act),
            mem((UNROLL, HP, width), act),
            mem((UNROLL, HP, width), bf16),
            mem((UNROLL, HP, width), bf16),
            mem((HP, CP), f32),
            mem((HP, CP), f32),
            mem((9, CP, 128), f32),
            mem((16, 128), f32),
            mem((13, CP, 128), f32),
            mem((128, 384), f32),
            mem((384, 128), f32),
            mem((CP, 16), bf16),
            mem((HP, CP), bf16),
            mem((CP, HP), bf16),
            mem((CP, HP), bf16),
            mem((HP, CP), bf16),
        ],
        compiler_params=pltpu.CompilerParams(vmem_limit_bytes=58 * MIB),
    )(
        inv, flags, blocks, rows, cols, cot, w_in, b_in[None], kernel, ln_gain[None], ln_bias[None], w_one, b_one[None],
        w_two, b_two[None],
    )


MESH = pl.DeviceIdType.MESH
MIB = 1024 * 1024
VM = pl.BlockSpec(memory_space=pltpu.VMEM)
SM = pl.BlockSpec(memory_space=pltpu.SMEM)
AXES = ("face", "tile")


def partial_kernel(pick_ref, slot_ref, source_ref, weight_ref, out_ref, part):
    count = weight_ref.shape[0]
    group = 8

    def one(i, _):
        for k in range(group):
            e = i * group + k
            x = jnp.dot(source_ref[pick_ref[e]], weight_ref[e], preferred_element_type=jnp.float32)
            part[e] = x.astype(jnp.bfloat16)
        return 0

    lax.fori_loop(0, count // group, one, 0)

    def put(d, _):
        out_ref[d, 0:16, :] = part[slot_ref[2 * d]]
        out_ref[d, 16:32, :] = part[slot_ref[2 * d + 1]]
        return 0

    lax.fori_loop(0, count, put, 0, unroll=8)


def partial_call(pick, slots, source, weight):
    count = weight.shape[0]
    return pl.pallas_call(
        partial_kernel,
        out_shape=jax.ShapeDtypeStruct((count, 32, 128), jnp.bfloat16),
        in_specs=[SM, SM, VM, VM],
        out_specs=VM,
        scratch_shapes=[pltpu.VMEM((count, 16, 128), jnp.bfloat16)],
        compiler_params=pltpu.CompilerParams(vmem_limit_bytes=32 * MIB),
    )(pick, slots, source, weight)


def exchange_kernel(faces, tiles, index, *refs):
    if index:
        ids_ref, box_ref, all_ref, got_ref, send, recv, local, send_a, recv_a, send_b, recv_b = refs
    else:
        box_ref, got_ref, send, recv, local = refs
    face = lax.axis_index("face")
    tile = lax.axis_index("tile")
    count = faces * tiles
    me = face * tiles + tile
    barrier = pltpu.get_barrier_semaphore()

    def greet(k, _):
        peer = lax.rem(me + k, count)
        pl.semaphore_signal(barrier, inc=1, device_id=(peer // tiles, lax.rem(peer, tiles)), device_id_type=MESH)
        return 0

    lax.fori_loop(1, count, greet, 0)
    pl.semaphore_wait(barrier, count - 1)

    if index:
        all_ref[face, tile] = ids_ref[...]
        first = []
        for k in range(1, tiles):
            first.append(
                pltpu.make_async_remote_copy(
                    src_ref=ids_ref,
                    dst_ref=all_ref.at[face, tile],
                    send_sem=send_a.at[k],
                    recv_sem=recv_a.at[k],
                    device_id=(face, lax.rem(tile + k, tiles)),
                    device_id_type=MESH,
                )
            )
            first[-1].start()

    def push(k, _):
        peer = lax.rem(me + k, count)
        pltpu.make_async_remote_copy(
            src_ref=box_ref.at[peer],
            dst_ref=got_ref.at[me],
            send_sem=send,
            recv_sem=recv,
            device_id=(peer // tiles, lax.rem(peer, tiles)),
            device_id_type=MESH,
        ).start()
        return 0

    lax.fori_loop(1, count, push, 0)
    own = pltpu.make_async_copy(box_ref.at[me], got_ref.at[me], local)
    own.start()
    if index:
        for copy in first:
            copy.wait()
        second = []
        for k in range(1, faces):
            second.append(
                pltpu.make_async_remote_copy(
                    src_ref=all_ref.at[face],
                    dst_ref=all_ref.at[face],
                    send_sem=send_b.at[k],
                    recv_sem=recv_b.at[k],
                    device_id=(lax.rem(face + k, faces), tile),
                    device_id_type=MESH,
                )
            )
            second[-1].start()
        for copy in second:
            copy.wait()
    own.wait()
    whole = pl.ds(0, count - 1)
    pltpu.make_async_copy(box_ref.at[whole], got_ref.at[whole], send).wait()
    pltpu.make_async_copy(box_ref.at[whole], got_ref.at[whole], recv).wait()


def exchange_call(box, ids, collective_id):
    faces, tiles = lax.axis_size("face"), lax.axis_size("tile")
    index = ids is not None
    out = [jax.ShapeDtypeStruct(box.shape, box.dtype)]
    args = [box]
    dma = pltpu.SemaphoreType.DMA
    scratch = [dma, dma, dma]
    if index:
        out = [jax.ShapeDtypeStruct((faces, tiles) + ids.shape, ids.dtype)] + out
        args = [ids] + args
        scratch += [dma((tiles,)), dma((tiles,)), dma((faces,)), dma((faces,))]
    return pl.pallas_call(
        functools.partial(exchange_kernel, faces, tiles, index),
        out_shape=tuple(out),
        in_specs=[VM] * len(args),
        out_specs=tuple([VM] * len(out)),
        scratch_shapes=scratch,
        compiler_params=pltpu.CompilerParams(
            collective_id=collective_id, has_side_effects=True, vmem_limit_bytes=32 * MIB
        ),
    )(*args)


def combine_kernel(label_ref, perm_ref, got_ref, out_ref, total):
    count = got_ref.shape[0]
    total[...] = jnp.zeros_like(total)

    def add(s, _):
        for k in range(2):
            spot = label_ref[2 * s + k]
            total[spot] += got_ref[s, 16 * k : 16 * k + 16, :].astype(jnp.float32)
        return 0

    lax.fori_loop(0, count, add, 0)

    def put(d, _):
        out_ref[d] = total[perm_ref[d]].astype(jnp.bfloat16)
        return 0

    lax.fori_loop(0, count, put, 0, unroll=8)


def combine_call(labels, perm, got):
    count = got.shape[0]
    return pl.pallas_call(
        combine_kernel,
        out_shape=jax.ShapeDtypeStruct((count, 16, 128), jnp.bfloat16),
        in_specs=[SM, SM, VM],
        out_specs=VM,
        scratch_shapes=[pltpu.VMEM((count + 1, 16, 128), jnp.float32)],
        compiler_params=pltpu.CompilerParams(vmem_limit_bytes=32 * MIB),
    )(labels, perm, got)


def lines_kernel(
    faces, tiles, inv_ref, link_ref, box_ref, rows_ref, cols_ref, edge, upper, lower, packet, packets, ends, line, wins,
    lots, windows, whole, send_v, recv_v, send_p, recv_p, send_e, recv_e, send_w, recv_w, send_l, recv_l,
):
    f32, bf16 = jnp.float32, jnp.bfloat16
    face = lax.axis_index("face")
    tile = lax.axis_index("tile")
    chans = box_ref.shape[1]
    nrow = box_ref.shape[0] // 4
    barrier = pltpu.get_barrier_semaphore()
    for k in range(1, tiles):
        pl.semaphore_signal(barrier, inc=1, device_id=(face, lax.rem(tile + k, tiles)), device_id_type=MESH)
    for k in range(1, faces):
        pl.semaphore_signal(barrier, inc=1, device_id=(lax.rem(face + k, faces), tile), device_id_type=MESH)
    pl.semaphore_wait(barrier, tiles + faces - 2)

    for k in range(4):
        edge[0, k] = box_ref[inv_ref[k]]
        edge[1, k] = box_ref[inv_ref[4 * nrow - 4 + k]]
    down = lax.rem(tile + 1, tiles)
    up = lax.rem(tile + tiles - 1, tiles)
    vertical = []
    for k, (dst, peer) in enumerate(((upper, down), (lower, up))):
        vertical.append(
            pltpu.make_async_remote_copy(
                src_ref=edge.at[1 - k],
                dst_ref=dst,
                send_sem=send_v.at[k],
                recv_sem=recv_v.at[k],
                device_id=(face, peer),
                device_id_type=MESH,
            )
        )
        vertical[-1].start()

    def end_copy(k, side):
        return pltpu.make_async_remote_copy(
            src_ref=edge.at[side],
            dst_ref=ends.at[side],
            send_sem=send_e.at[k],
            recv_sem=recv_e.at[side],
            device_id=(face, lax.rem(tile + k, tiles)),
            device_id_type=MESH,
        )

    for side, owner in ((0, 0), (1, tiles - 1)):

        @pl.when(tile == owner)
        def _():
            for k in range(1, tiles):
                end_copy(k, side).start()
            ends[side] = edge[side]

    lane = lax.broadcasted_iota(jnp.int32, (chans, 128), 1)

    def pick(r, acc):
        left = pltpu.roll(box_ref[inv_ref[4 * r]].astype(f32), r, 1)
        right = pltpu.roll(box_ref[inv_ref[4 * r + 3]].astype(f32), r + nrow + 1, 1)
        return jnp.where(lane == r, left, jnp.where(lane == r + nrow, right, acc))

    packet[...] = lax.fori_loop(0, nrow, pick, jnp.zeros((chans, 128), f32), unroll=8).astype(bf16)
    packets[tile] = packet[...]
    sends = []
    for k in range(1, tiles):
        sends.append(
            pltpu.make_async_remote_copy(
                src_ref=packet,
                dst_ref=packets.at[tile],
                send_sem=send_p.at[k],
                recv_sem=recv_p.at[k],
                device_id=(face, lax.rem(tile + k, tiles)),
                device_id_type=MESH,
            )
        )
        sends[-1].start()
    for copy in sends:
        copy.wait()
    for side, owner in ((0, 0), (1, tiles - 1)):

        @pl.when(tile == owner)
        def _():
            for k in range(1, tiles):
                end_copy(k, side).wait_send()

        @pl.when(tile != owner)
        def _():
            end_copy(1, side).wait_recv()

    per = 128 // nrow
    for side in range(2):
        line[side] = jnp.concatenate([ends[side, k] for k in range(4)], axis=1).astype(f32)
        parts = []
        for block in range(tiles // per):
            acc = jnp.zeros((chans, 128), f32)
            for i in range(per):
                seg = packets[block * per + i].astype(f32)
                seg = pltpu.roll(seg, (128 + (i - side) * nrow) % 128, 1) if i != side else seg
                acc = jnp.where((lane >= i * nrow) & (lane < (i + 1) * nrow), seg, acc)
            parts.append(acc)
        line[2 + side] = jnp.concatenate(parts, axis=1)
    width = tiles * nrow
    for s in range(4):
        full = line[s]
        for k in range(4):
            lots[s, k] = full[:, k * 128 : (k + 1) * 128].astype(bf16)
        near = pltpu.roll(full, lax.rem(width + 1 - tile * nrow, width), 1)[:, 0:128]
        far = pltpu.roll(full, lax.rem(width + 65 - (tiles - 1 - tile) * nrow, width), 1)[:, 0:128]
        wins[s] = jnp.where(lane < 64, near, far).astype(bf16)
    windows[face] = wins[...]
    sends = []
    for k in range(1, faces):
        sends.append(
            pltpu.make_async_remote_copy(
                src_ref=wins,
                dst_ref=windows.at[face],
                send_sem=send_w.at[k],
                recv_sem=recv_w.at[k],
                device_id=(lax.rem(face + k, faces), tile),
                device_id_type=MESH,
            )
        )
        sends[-1].start()

    def lot_copy(k):
        return pltpu.make_async_remote_copy(
            src_ref=lots,
            dst_ref=whole.at[face],
            send_sem=send_l.at[k],
            recv_sem=recv_l.at[k],
            device_id=(lax.rem(face + k, faces), tile),
            device_id_type=MESH,
        )

    at_end = (tile == 0) | (tile == tiles - 1)

    @pl.when(at_end)
    def _():
        for k in range(1, faces):
            lot_copy(k).start()
        whole[face] = lots[...]

    for copy in vertical:
        copy.wait()
    for copy in sends:
        copy.wait()
    row = lax.broadcasted_iota(jnp.int32, (128, 128), 0)
    col = lax.broadcasted_iota(jnp.int32, (128, 128), 1)
    at = 4 * (face * 3)
    for side in range(2):
        base = (face * 4 + 2 + side) * 3
        view = windows[link_ref[base], link_ref[base + 1]]
        spot = jnp.where(link_ref[base + 2] == 1, 65 + nrow - col, col)
        turn = (row == spot).astype(bf16)
        cols_ref[side] = jnp.dot(view, turn, preferred_element_type=f32).astype(bf16)
        rows_ref[side] = (upper, lower)[side][...]

    @pl.when(at_end)
    def _():
        for k in range(1, faces):
            lot_copy(k).wait()

    for side, owner in ((0, 0), (1, tiles - 1)):

        @pl.when(tile == owner)
        def _():
            base = (face * 4 + side) * 3
            flip = link_ref[base + 2] == 1
            turn = (row == jnp.where(flip, 127 - col, col)).astype(bf16)
            for k in range(4):
                view = whole[link_ref[base], link_ref[base + 1], jnp.where(flip, 3 - k, k)]
                rows_ref[side, k] = jnp.dot(view, turn, preferred_element_type=f32).astype(bf16)


def lines_call(inv, links, box, collective_id):
    faces, tiles = lax.axis_size("face"), lax.axis_size("tile")
    dma = pltpu.SemaphoreType.DMA
    bf16 = jnp.bfloat16
    chans = box.shape[1]
    block = (4, chans, 128)
    return pl.pallas_call(
        functools.partial(lines_kernel, faces, tiles),
        out_shape=(jax.ShapeDtypeStruct((2,) + block, bf16), jax.ShapeDtypeStruct((2, chans, 128), bf16)),
        in_specs=[SM, SM, VM],
        out_specs=(VM, VM),
        scratch_shapes=[
            pltpu.VMEM((2,) + block, bf16),
            pltpu.VMEM(block, bf16),
            pltpu.VMEM(block, bf16),
            pltpu.VMEM((chans, 128), bf16),
            pltpu.VMEM((tiles, chans, 128), bf16),
            pltpu.VMEM((2,) + block, bf16),
            pltpu.VMEM((4, chans, 512), jnp.float32),
            pltpu.VMEM(block, bf16),
            pltpu.VMEM((4,) + block, bf16),
            pltpu.VMEM((faces,) + block, bf16),
            pltpu.VMEM((faces, 4) + block, bf16),
            dma((2,)), dma((2,)), dma((tiles,)), dma((tiles,)), dma((tiles,)), dma((2,)), dma((faces,)), dma((faces,)),
            dma((faces,)), dma((faces,)),
        ],
        compiler_params=pltpu.CompilerParams(
            collective_id=collective_id, has_side_effects=True, vmem_limit_bytes=32 * MIB
        ),
    )(inv, links, box)


def reduce_kernel(
    faces, tiles, grad_ref, one_ref, two_ref, ker_ref, first, part, second, mine, full, send_a, recv_a, send_b, recv_b,
    send_c, recv_c,
):
    face = lax.axis_index("face")
    tile = lax.axis_index("tile")
    size = grad_ref.shape[0] // tiles
    barrier = pltpu.get_barrier_semaphore()
    for k in range(1, tiles):
        pl.semaphore_signal(barrier, inc=1, device_id=(face, lax.rem(tile + k, tiles)), device_id_type=MESH)
    for k in range(1, faces):
        pl.semaphore_signal(barrier, inc=1, device_id=(lax.rem(face + k, faces), tile), device_id_type=MESH)
    pl.semaphore_wait(barrier, tiles + faces - 2)

    def spot(t):
        return pl.ds(pl.multiple_of(t * size, 8), size)

    copies = []
    for k in range(1, tiles):
        peer = lax.rem(tile + k, tiles)
        copies.append(
            pltpu.make_async_remote_copy(
                src_ref=grad_ref.at[spot(peer)],
                dst_ref=first.at[k],
                send_sem=send_a.at[k],
                recv_sem=recv_a.at[k],
                device_id=(face, peer),
                device_id_type=MESH,
            )
        )
        copies[-1].start()
    total = grad_ref[spot(tile), :]
    for k in range(1, tiles):
        copies[k - 1].wait_recv()
        total = total + first[k]
    part[...] = total
    second[face] = total
    later = []
    for k in range(1, faces):
        later.append(
            pltpu.make_async_remote_copy(
                src_ref=part,
                dst_ref=second.at[face],
                send_sem=send_b.at[k],
                recv_sem=recv_b.at[k],
                device_id=(lax.rem(face + k, faces), tile),
                device_id_type=MESH,
            )
        )
        later[-1].start()
    for copy in later:
        copy.wait_recv()
    total = second[0]
    for k in range(1, faces):
        total = total + second[k]
    mine[...] = total
    full[spot(tile), :] = total
    last = []
    for k in range(1, tiles):
        last.append(
            pltpu.make_async_remote_copy(
                src_ref=mine,
                dst_ref=full.at[spot(tile)],
                send_sem=send_c.at[k],
                recv_sem=recv_c.at[k],
                device_id=(face, lax.rem(tile + k, tiles)),
                device_id_type=MESH,
            )
        )
        last[-1].start()
    for copy in last:
        copy.wait_recv()
    two_ref[...] = full[0:360, 0:90]
    one_ref[...] = full[360:720, 0:128].T[0:90, :]
    ker_ref[...] = full[720:729, 0:90]
    for copy in copies + later + last:
        copy.wait_send()


def reduce_call(grad, collective_id):
    faces, tiles = lax.axis_size("face"), lax.axis_size("tile")
    dma = pltpu.SemaphoreType.DMA
    f32 = jnp.float32
    size = grad.shape[0] // tiles
    return pl.pallas_call(
        functools.partial(reduce_kernel, faces, tiles),
        out_shape=(
            jax.ShapeDtypeStruct((90, 360), f32),
            jax.ShapeDtypeStruct((360, 90), f32),
            jax.ShapeDtypeStruct((9, 90), f32),
        ),
        in_specs=[VM],
        out_specs=(VM, VM, VM),
        scratch_shapes=[
            pltpu.VMEM((tiles, size, 128), f32),
            pltpu.VMEM((size, 128), f32),
            pltpu.VMEM((faces, size, 128), f32),
            pltpu.VMEM((size, 128), f32),
            pltpu.VMEM(grad.shape, f32),
            dma((tiles,)), dma((tiles,)), dma((faces,)), dma((faces,)), dma((tiles,)), dma((tiles,)),
        ],
        compiler_params=pltpu.CompilerParams(
            collective_id=collective_id, has_side_effects=True, vmem_limit_bytes=32 * MIB
        ),
    )(grad)


def remap(source, entry_block, entry_source, entry_weight, lat_to_nested):
    count = entry_block.shape[0]
    me = lax.axis_index("face") * lax.axis_size("tile") + lax.axis_index("tile")
    ids = jnp.arange(count, dtype=jnp.int32)
    owner = entry_block // count
    hit = owner[None, :] == ids[:, None]
    low = jnp.min(jnp.where(hit, ids[None, :], count - 1), axis=1)
    high = jnp.max(jnp.where(hit, ids[None, :], 0), axis=1)
    slots = jnp.stack([low, high], axis=1).reshape(-1)
    perm = jnp.sum(jnp.where((lat_to_nested // count)[None, :] == ids[:, None], ids[None, :], 0), axis=1)
    box = partial_call(entry_source, slots, source, entry_weight)
    table, got = exchange_call(box, jnp.stack([entry_block, lat_to_nested]), 1)
    table = table.reshape(count, 2, count)
    key = ids[None, :] * count + table[:, 0] % count
    hit = table[:, 0] // count == me
    low = jnp.min(jnp.where(hit, key, count * count), axis=1)
    high = jnp.max(jnp.where(hit, key, -1), axis=1)
    label_low = jnp.where(high >= 0, low % count, count)
    label_high = jnp.where(high > low, high % count, count)
    labels = jnp.stack([label_low, label_high], axis=1).reshape(-1)
    spots = jnp.sum(jnp.where(table[:, 1] // count == me, table[:, 1] % count, 0), axis=1)
    inv = jnp.sum(jnp.where(spots[None, :] == ids[:, None], ids[None, :], 0), axis=1)
    out = combine_call(labels, perm, got)
    return inv, exchange_call(out, None, 2)[0]

def per_device(
    source, entry_block, entry_source, entry_weight, lat_to_nested, face_links, w_in, b_in, kernel, ln_gain, ln_bias,
    w_one, b_one, w_two, b_two, cotangent,
):
    tile_at = lax.axis_index("tile")
    face_count, tile_count = lax.axis_size("face"), lax.axis_size("tile")
    width = cotangent.shape[3]
    inv, box = remap(source, entry_block, entry_source, entry_weight, lat_to_nested)
    rows, cols = lines_call(inv, face_links.reshape(-1), box, 3)
    flags = jnp.stack([tile_at == 0, tile_at == tile_count - 1]).astype(jnp.int32)
    scale = 1.0 / math.sqrt(face_count * width * width)
    output, grad = strip_call(
        inv, flags, box, rows, cols, cotangent[0], w_in, b_in, kernel, ln_gain, ln_bias, w_one, b_one, w_two, b_two,
        scale,
    )
    grad_one, grad_two, grad_kernel = reduce_call(grad, 4)
    return (output[None], grad_one, grad_two, grad_kernel)


def solution(mesh):
    split = P(("face", "tile"))
    strips = P("face", None, "tile", None)
    return jax.shard_map(
        per_device,
        mesh=mesh,
        in_specs=(split,) * 5 + (P(),) * 10 + (strips,),
        out_specs=(strips, P(), P(), P()),
        check_vma=False,
    )
```

```python
import functools
import math

import jax
import jax.numpy as jnp
from jax import lax
from jax.experimental import pallas as pl
from jax.experimental.pallas import tpu as pltpu
from jax.sharding import PartitionSpec as P


GELU_K = 0.7978845608028654
GELU_C = 0.044715
NORM_EPS = 1e-06
CP = 96
HP = 368
PITCH = 40
UNROLL = 2
HID = 16
MIB = 1024 * 1024


def strip_kernel(
    blocks_ref, rows_ref, cols_ref, cot_ref, win_ref, bin_ref, ker_ref, gain_ref, bias_ref, wone_ref,
    bone_ref, wtwo_ref, btwo_ref, out_ref, grad_ref, field, cols, depth, cot_s, out_s, scaled_s, norm_s, cotb_s,
    pre_s, back_s, hid_s, bp_s, g2_s, g1_s, gk_s, tab_s, vec_s, flat_s, w_in_s, w1t_s, w1_s, w2t_s, w2_s, scale,
):
    chans, rows, width = cot_ref.shape
    hidden = wone_ref.shape[1]
    lanes = width // 128
    f32, bf16 = jnp.float32, jnp.bfloat16
    nt = (((1,), (1,)), ((), ()))

    def wide(v):
        return jnp.concatenate([v] * lanes, axis=1)

    tab_s[...] = jnp.zeros_like(tab_s)
    for j, ref in enumerate((bin_ref, gain_ref, bias_ref, btwo_ref)):
        tab_s[j : j + 1, 0:chans] = ref[...]
    tab_s[4:13, 0:chans] = ker_ref[...]
    turned = tab_s[...].T
    for j in range(13):
        vec_s[j] = jnp.broadcast_to(turned[0:CP, j : j + 1], (CP, 128))
    tab_s[...] = jnp.zeros_like(tab_s)
    tab_s[0:16, 0:chans] = win_ref[...].astype(f32)
    w_in_s[...] = tab_s[...].T[0:CP, 0:16].astype(bf16)
    flat_s[...] = jnp.zeros_like(flat_s)
    flat_s[0:chans, 0:hidden] = wone_ref[...].astype(f32)
    w1_s[...] = flat_s[0:CP, 0:HP].astype(bf16)
    high = bone_ref[...].astype(bf16).astype(f32)
    flat_s[chans : chans + 1, 0:hidden] = high
    flat_s[chans + 1 : chans + 2, 0:hidden] = bone_ref[...] - high
    w1t_s[...] = (flat_s[...].T[0:HP, 0:CP] * 0.5).astype(bf16)
    flat_s[...] = jnp.zeros_like(flat_s)
    flat_s[0:chans, 0:hidden] = wtwo_ref[...].astype(f32)
    w2t_s[...] = flat_s[0:CP, 0:HP].astype(bf16)
    w2_s[...] = (flat_s[...].T[0:HP, 0:CP] * 0.5).astype(bf16)

    tile, tile_count = lax.axis_index("tile"), lax.axis_size("tile")
    lane = lax.broadcasted_iota(jnp.int32, (CP, 128), 1)
    last = lane == jnp.where(tile == tile_count - 1, rows + 1, -1)
    first = lane == jnp.where(tile == 0, 0, -1)
    for side in range(2):
        v = jnp.dot(w_in_s[...], cols_ref[side], preferred_element_type=f32) + vec_s[0]
        cols[side] = jnp.where(first | last, 0.0, v.astype(bf16).astype(f32))

    g2_s[...] = jnp.zeros_like(g2_s)
    g1_s[...] = jnp.zeros_like(g1_s)
    cot_s[:, chans * PITCH :, :] = jnp.zeros((lanes, (CP + 1 - chans) * PITCH, 128), f32)

    def turn(c, _):
        x = cot_ref[c].astype(f32)
        for k in range(lanes):
            cot_s[k, pl.ds(pl.multiple_of(c * PITCH, 8), rows), :] = x[:, k * 128 : (k + 1) * 128]
        return 0

    lax.fori_loop(0, chans, turn, 0, unroll=2)

    def make_row(at, x):
        lat = jnp.dot(w_in_s[...], x, preferred_element_type=f32) + wide(vec_s[0])
        lat = lat.astype(bf16).astype(f32)
        wide_lane = lax.broadcasted_iota(jnp.int32, (CP, 128), 1)
        mid = [lat[:, k * 128 : (k + 1) * 128] for k in range(lanes)]
        up = [pltpu.roll(cols[0], lax.rem(128 - at, 128), 1)] + [pltpu.roll(m, 1, 1) for m in mid]
        dn = [pltpu.roll(m, 127, 1) for m in mid] + [pltpu.roll(cols[1], 127 - at, 1)]
        for k in range(lanes):
            part = slice(k * 128, (k + 1) * 128)
            field[at, 0, :, part] = jnp.where(wide_lane == 0, up[k], up[k + 1])
            field[at, 1, :, part] = mid[k]
            field[at, 2, :, part] = jnp.where(wide_lane == 127, dn[k + 1], dn[k])

    make_row(0, jnp.concatenate([rows_ref[0, k] for k in range(lanes)], axis=1))
    make_row(rows + 1, jnp.concatenate([rows_ref[1, k] for k in range(lanes)], axis=1))

    def row_step(r, _):
        make_row(r + 1, jnp.concatenate([blocks_ref[r * lanes + k] for k in range(lanes)], axis=1))
        return 0

    lax.fori_loop(0, rows, row_step, 0, unroll=2)

    def shifted(r, c):
        return [
            [field[r, side, pl.ds(c, 8), k * 128 : (k + 1) * 128] for k in range(lanes)] for side in range(3)
        ]

    def conv_chunk(i, _):
        c = pl.multiple_of(i * 8, 8)
        w = [vec_s[4 + tap, pl.ds(c, 8), :] for tap in range(9)]

        def mix(a, views, k):
            return w[3 * a] * views[0][k] + w[3 * a + 1] * views[1][k] + w[3 * a + 2] * views[2][k]

        v0, v1 = shifted(0, c), shifted(1, c)
        one = tuple(mix(0, v0, k) + mix(1, v1, k) for k in range(lanes))
        two = tuple(mix(0, v1, k) for k in range(lanes))

        def go(r, carry):
            one, two = carry
            v = shifted(r + 2, c)
            for k in range(lanes):
                depth[r, pl.ds(c, 8), k * 128 : (k + 1) * 128] = one[k] + mix(2, v, k)
            return (
                tuple(two[k] + mix(1, v, k) for k in range(lanes)),
                tuple(mix(0, v, k) for k in range(lanes)),
            )

        lax.fori_loop(0, rows, go, (one, two), unroll=4)
        return 0

    lax.fori_loop(0, CP // 8, conv_chunk, 0)

    row_id = lax.broadcasted_iota(jnp.int32, (CP, 128), 0)
    real = row_id < chans
    ones_rows = (row_id == chans) | (row_id == chans + 1)

    def col_sum(v):
        return jnp.sum(v, axis=0, keepdims=True)

    def front(r, u):
        stds = []
        for k in range(lanes):
            part = slice(k * 128, (k + 1) * 128)
            d = depth[r, :, part]
            d = d - col_sum(d) * (1.0 / chans)
            d = jnp.where(real, d, 0.0)
            inv_std = lax.rsqrt(col_sum(d * d) * (1.0 / chans) + NORM_EPS)
            s = d * inv_std
            scaled_s[u, :, part] = s
            n = jnp.where(ones_rows, 1.0, s * vec_s[1] + vec_s[2])
            norm_s[u, :, part] = n.astype(bf16)
            cotb_s[u, :, part] = cot_s[k, pl.ds(r, CP, stride=PITCH), :].astype(bf16)
            stds.append(inv_std)
        pre_s[u] = jnp.dot(w1t_s[...], norm_s[u], preferred_element_type=f32).astype(pre_s.dtype)
        back_s[u] = jnp.dot(w2_s[...], cotb_s[u], preferred_element_type=f32).astype(back_s.dtype)
        return stds

    def middle(u):
        ty = pre_s.dtype
        num = lambda v: jnp.asarray(v, ty)
        for h in range(0, HP, 16):
            x = pre_s[u, h : h + 16, :]
            q = x * x
            t = jnp.tanh(x * (num(2.0 * GELU_K) + num(8.0 * GELU_K * GELU_C) * q))
            p = num(1.0) + t
            g = x * p
            slope = p + g * (num(1.0) - t) * (num(2.0 * GELU_K) + num(24.0 * GELU_K * GELU_C) * q)
            hid_s[u, h : h + 16, :] = g.astype(bf16)
            bp_s[u, h : h + 16, :] = (back_s[u, h : h + 16, :] * slope).astype(bf16)

    def rear(r, u, stds):
        out = jnp.dot(w2t_s[...], hid_s[u], preferred_element_type=f32)
        hat = jnp.dot(w1_s[...], bp_s[u], preferred_element_type=f32)
        for k in range(lanes):
            part = slice(k * 128, (k + 1) * 128)
            out_s[k, pl.ds(r, CP, stride=PITCH), :] = out[:, part] + vec_s[3] + field[r + 1, 1, :, part]
            b = hat[:, part] * vec_s[1]
            s = scaled_s[u, :, part]
            one = col_sum(b) * (stds[k] * (1.0 / chans))
            two = col_sum(b * s) * (stds[k] * (1.0 / chans))
            depth[r, :, part] = b * stds[k] - one - s * two

    def step(i, _):
        stds = [front(i * UNROLL + u, u) for u in range(UNROLL)]
        for u in range(UNROLL):
            middle(u)
        for u in range(UNROLL):
            rear(i * UNROLL + u, u, stds[u])
        g2_s[...] += sum(lax.dot_general(hid_s[u], cotb_s[u], nt, preferred_element_type=f32) for u in range(UNROLL))
        g1_s[...] += sum(lax.dot_general(bp_s[u], norm_s[u], nt, preferred_element_type=f32) for u in range(UNROLL))
        return 0

    lax.fori_loop(0, rows // UNROLL, step, 0)

    def back(c, _):
        x = jnp.concatenate([out_s[k, pl.ds(pl.multiple_of(c * PITCH, 8), rows), :] for k in range(lanes)], axis=1)
        out_ref[c] = x.astype(bf16)
        return 0

    lax.fori_loop(0, chans, back, 0, unroll=2)

    def kernel_chunk(i, _):
        c = pl.multiple_of(i * 8, 8)

        def grad_row(r):
            return tuple(depth[r, pl.ds(c, 8), k * 128 : (k + 1) * 128] for k in range(lanes))

        def fold(acc, a, b, views):
            new = list(acc)
            for s in range(3):
                m = b[0] * views[s][0]
                for k in range(1, lanes):
                    m = m + b[k] * views[s][k]
                new[3 * a + s] = new[3 * a + s] + m
            return tuple(new)

        acc = tuple(jnp.zeros((8, 128), f32) for _ in range(9))
        b0 = grad_row(0)
        acc = fold(acc, 0, b0, shifted(0, c))
        b1 = grad_row(1)
        v = shifted(1, c)
        acc = fold(fold(acc, 0, b1, v), 1, b0, v)

        def go(r, carry):
            acc, b1, b0 = carry
            v = shifted(r, c)
            b = grad_row(r)
            acc = fold(fold(fold(acc, 0, b, v), 1, b1, v), 2, b0, v)
            return acc, b, b1

        acc, b1, b0 = lax.fori_loop(2, rows, go, (acc, b1, b0), unroll=3)
        v = shifted(rows, c)
        acc = fold(fold(acc, 1, b1, v), 2, b0, v)
        acc = fold(acc, 2, b1, shifted(rows + 1, c))
        for tap in range(9):
            gk_s[tap, pl.ds(c, 8), :] = acc[tap]
        return 0

    lax.fori_loop(0, CP // 8, kernel_chunk, 0)
    grad_ref[360:384, :] = jnp.zeros((24, 128), f32)
    grad_ref[744:768, :] = jnp.zeros((24, 128), f32)
    grad_ref[0:hidden, 0:CP] = g2_s[0:hidden, :] * scale
    grad_ref[384 : 384 + hidden, 0:CP] = g1_s[0:hidden, :] * scale
    ones = jnp.ones((8, 128), f32)
    for tap in range(9):
        line = lax.dot_general(ones, gk_s[tap], nt, preferred_element_type=f32, precision=lax.Precision.HIGHEST)
        grad_ref[368 + tap : 369 + tap, 0:CP] = line[0:1, :] * scale


def strip_call(blocks, rows, cols, cot, w_in, b_in, kernel, ln_gain, ln_bias, w_one, b_one, w_two, b_two, scale):
    chans, nrow, width = cot.shape
    f32, bf16 = jnp.float32, jnp.bfloat16
    lanes = width // 128
    act = bf16 if HID == 16 else f32
    vm = pl.BlockSpec(memory_space=pltpu.VMEM)
    mem = pltpu.VMEM
    return pl.pallas_call(
        functools.partial(strip_kernel, scale=scale),
        out_shape=(jax.ShapeDtypeStruct((chans, nrow, width), bf16), jax.ShapeDtypeStruct((768, 128), f32)),
        in_specs=[vm] * 13,
        out_specs=(vm, vm),
        scratch_shapes=[
            mem((nrow + 2, 3, CP, width), f32),
            mem((2, CP, 128), f32),
            mem((nrow, CP, width), f32),
            mem((lanes, CP * PITCH + PITCH, 128), f32),
            mem((lanes, CP * PITCH + PITCH, 128), f32),
            mem((UNROLL, CP, width), f32),
            mem((UNROLL, CP, width), bf16),
            mem((UNROLL, CP, width), bf16),
            mem((UNROLL, HP, width), act),
            mem((UNROLL, HP, width), act),
            mem((UNROLL, HP, width), bf16),
            mem((UNROLL, HP, width), bf16),
            mem((HP, CP), f32),
            mem((HP, CP), f32),
            mem((9, CP, 128), f32),
            mem((16, 128), f32),
            mem((13, CP, 128), f32),
            mem((128, 384), f32),
            mem((CP, 16), bf16),
            mem((HP, CP), bf16),
            mem((CP, HP), bf16),
            mem((CP, HP), bf16),
            mem((HP, CP), bf16),
        ],
        compiler_params=pltpu.CompilerParams(vmem_limit_bytes=60 * MIB),
    )(
        blocks, rows, cols, cot, w_in, b_in[None], kernel, ln_gain[None], ln_bias[None], w_one, b_one[None],
        w_two.T, b_two[None],
    )


MESH = pl.DeviceIdType.MESH
MIB = 1024 * 1024
VMEM_BYTES = 60 * MIB
VM = pl.BlockSpec(memory_space=pltpu.VMEM)
SM = pl.BlockSpec(memory_space=pltpu.SMEM)
AXES = ("face", "tile")


def remap_kernel(
    faces, tiles, pick_ref, link_ref, entry_ref, nested_ref, source_ref, weight_ref, placed_ref, rows_ref, cols_ref, weight,
    part, box, got, table, block_of, nest_of, wide_s, narrow_s, box2, got2, edge, upper, lower, packet, packets, ends,
    line, wins, lots, chosen, windows, whole, ids, slot_v, slot_s, send_w, send_s, send_1, recv_1, local, send_2, recv_2, send_ia, recv_ia, send_ib, recv_ib,
    send_v, recv_v, send_p, recv_p, send_e, recv_e, send_n, recv_n, send_l, recv_l,
):
    f32, bf16 = jnp.float32, jnp.bfloat16
    face = lax.axis_index("face")
    tile = lax.axis_index("tile")
    count = faces * tiles
    me = face * tiles + tile
    chans = source_ref.shape[1]
    nrow = count // 4
    loads = weight_ref.shape[0] // 4

    def load(k):
        span = pl.ds(k * loads, loads)
        return pltpu.make_async_copy(weight_ref.at[span], weight.at[span], send_w.at[k])

    for k in range(4):
        load(k).start()
    barrier = pltpu.get_barrier_semaphore()

    def greet(k, _):
        peer = lax.rem(me + k, count)
        pl.semaphore_signal(barrier, inc=1, device_id=(peer // tiles, lax.rem(peer, tiles)), device_id_type=MESH)
        return 0

    lax.fori_loop(1, count, greet, 0)

    row = lax.broadcasted_iota(jnp.int32, (count, count), 0)
    col = lax.broadcasted_iota(jnp.int32, (count, count), 1)

    def turned(v):
        return jnp.broadcast_to(v, (count, count)).T

    ids[0:1, :] = entry_ref[...]
    ids[1:2, :] = nested_ref[...]
    hit = (jnp.broadcast_to(entry_ref[...], (count, count)) >> 7) == row
    fcol = col.astype(f32)
    low = turned(jnp.min(jnp.where(hit, fcol, float(count - 1)), axis=1, keepdims=True))
    high = turned(jnp.max(jnp.where(hit, fcol, 0.0), axis=1, keepdims=True))
    slot_v[...] = jnp.where(row[0:8] == 0, low[0:8], high[0:8]).astype(jnp.int32)
    to_scalars = pltpu.make_async_copy(slot_v, slot_s, send_s)
    to_scalars.start()

    group = 8
    for k in range(4):
        load(k).wait()

        def multiply(i, _):
            for j in range(group):
                e = k * loads + i * group + j
                x = jnp.dot(source_ref[pick_ref[e]], weight[e], preferred_element_type=f32)
                part[e] = x.astype(bf16)
            return 0

        lax.fori_loop(0, loads // group, multiply, 0)

    to_scalars.wait()

    def fill(d, _):
        box[d, 0:16, :] = part[slot_s[0, d] & (count - 1)]
        box[d, 16:32, :] = part[slot_s[1, d] & (count - 1)]
        return 0

    lax.fori_loop(0, count, fill, 0, unroll=8)
    table[face, tile] = ids[...]
    pl.semaphore_wait(barrier, count - 1)

    index = []
    for k in range(1, tiles):
        index.append(
            pltpu.make_async_remote_copy(
                src_ref=ids,
                dst_ref=table.at[face, tile],
                send_sem=send_ia.at[k],
                recv_sem=recv_ia.at[k],
                device_id=(face, lax.rem(tile + k, tiles)),
                device_id_type=MESH,
            )
        )
        index[-1].start()

    def exchange(src, dst, send, recv):
        def push(k, _):
            peer = lax.rem(me + k, count)
            pltpu.make_async_remote_copy(
                src_ref=src.at[peer],
                dst_ref=dst.at[me],
                send_sem=send,
                recv_sem=recv,
                device_id=(peer // tiles, lax.rem(peer, tiles)),
                device_id_type=MESH,
            ).start()
            return 0

        lax.fori_loop(1, count, push, 0, unroll=2)
        own = pltpu.make_async_copy(src.at[me], dst.at[me], local)
        own.start()
        return own

    def arrive(own, src, dst, recv):
        whole_box = pl.ds(0, count - 1)
        own.wait()
        pltpu.make_async_copy(src.at[whole_box], dst.at[whole_box], recv).wait()

    own = exchange(box, got, send_1, recv_1)
    for copy in index:
        copy.wait()
    index = []
    for k in range(1, faces):
        index.append(
            pltpu.make_async_remote_copy(
                src_ref=table.at[face],
                dst_ref=table.at[face],
                send_sem=send_ib.at[k],
                recv_sem=recv_ib.at[k],
                device_id=(lax.rem(face + k, faces), tile),
                device_id_type=MESH,
            )
        )
        index[-1].start()
    for copy in index:
        copy.wait()

    def spread(f, _):
        for t in range(tiles):
            pair = table[f, t]
            block_of[pl.ds(f * tiles + t, 1), :] = pair[0:1, :]
            nest_of[pl.ds(f * tiles + t, 1), :] = pair[1:2, :]
        return 0

    lax.fori_loop(0, faces, spread, 0)
    blocks = block_of[...]
    hit = (blocks >> 7) == me
    key = (col * count + (blocks & (count - 1))).astype(f32)
    low = jnp.min(jnp.where(hit, key, 1e9), axis=1, keepdims=True)
    high = jnp.max(jnp.where(hit, key, -1.0), axis=1, keepdims=True)
    low_label = jnp.where(high >= 0.0, low.astype(jnp.int32) & (count - 1), -1).astype(f32)
    high_label = jnp.where(high > low, high.astype(jnp.int32) & (count - 1), -1).astype(f32)
    nest = jnp.broadcast_to(nested_ref[...], (count, count))
    perm = jnp.sum(jnp.where((nest >> 7) == row, col.astype(f32), 0.0), axis=1, keepdims=True)
    take_low = (turned(low_label) == perm).astype(f32).astype(bf16)
    take_high = (turned(high_label) == perm).astype(f32).astype(bf16)
    nest = nest_of[...]
    spot = jnp.sum(jnp.where((nest >> 7) == me, (nest & (count - 1)).astype(f32), 0.0), axis=1, keepdims=True)
    place = (turned(spot) == row.astype(f32)).astype(f32).astype(bf16)

    arrive(own, box, got, recv_1)
    deep = 40

    def widen(s, _):
        wide_s[pl.ds(pl.multiple_of(s * deep, 8), 32), :] = got[s].astype(f32)
        return 0

    lax.fori_loop(0, count, widen, 0, unroll=8)
    pitch = 24
    for c in range(chans):
        one = wide_s[pl.ds(c, count, stride=deep), :].astype(bf16)
        two = wide_s[pl.ds(16 + c, count, stride=deep), :].astype(bf16)
        y = jnp.dot(take_low, one, preferred_element_type=f32) + jnp.dot(take_high, two, preferred_element_type=f32)
        narrow_s[pl.ds(c, count, stride=pitch), :] = y

    def narrow(d, _):
        box2[d] = narrow_s[pl.ds(pl.multiple_of(d * pitch, 8), 16), :].astype(bf16)
        return 0

    lax.fori_loop(0, count, narrow, 0, unroll=8)
    own = exchange(box2, got2, send_2, recv_2)
    arrive(own, box2, got2, recv_2)

    def widen_two(s, _):
        wide_s[pl.ds(pl.multiple_of(s * pitch, 8), 16), :] = got2[s].astype(f32)
        return 0

    lax.fori_loop(0, count, widen_two, 0, unroll=8)
    for c in range(chans):
        one = wide_s[pl.ds(c, count, stride=pitch), :].astype(bf16)
        narrow_s[pl.ds(c, count, stride=pitch), :] = jnp.dot(place, one, preferred_element_type=f32)

    def settle(m, _):
        placed_ref[m] = narrow_s[pl.ds(pl.multiple_of(m * pitch, 8), 16), :].astype(bf16)
        return 0

    lax.fori_loop(0, count, settle, 0, unroll=8)

    for k in range(4):
        edge[0, k] = placed_ref[k]
        edge[1, k] = placed_ref[4 * nrow - 4 + k]
    down = lax.rem(tile + 1, tiles)
    up = lax.rem(tile + tiles - 1, tiles)
    vertical = []
    for k, (dst, peer) in enumerate(((upper, down), (lower, up))):
        vertical.append(
            pltpu.make_async_remote_copy(
                src_ref=edge.at[1 - k],
                dst_ref=dst,
                send_sem=send_v.at[k],
                recv_sem=recv_v.at[k],
                device_id=(face, peer),
                device_id_type=MESH,
            )
        )
        vertical[-1].start()

    def end_copy(k, side):
        return pltpu.make_async_remote_copy(
            src_ref=edge.at[side],
            dst_ref=ends.at[side],
            send_sem=send_e.at[k],
            recv_sem=recv_e.at[side],
            device_id=(face, lax.rem(tile + k, tiles)),
            device_id_type=MESH,
        )

    for side, owner in ((0, 0), (1, tiles - 1)):

        @pl.when(tile == owner)
        def _():
            for k in range(1, tiles):
                end_copy(k, side).start()
            ends[side] = edge[side]

    lane = lax.broadcasted_iota(jnp.int32, (chans, 128), 1)

    def pick(r, acc):
        left = pltpu.roll(placed_ref[4 * r].astype(f32), r, 1)
        right = pltpu.roll(placed_ref[4 * r + 3].astype(f32), r + nrow + 1, 1)
        return jnp.where(lane == r, left, jnp.where(lane == r + nrow, right, acc))

    packet[...] = lax.fori_loop(0, nrow, pick, jnp.zeros((chans, 128), f32), unroll=8).astype(bf16)
    packets[tile] = packet[...]
    sends = []
    for k in range(1, tiles):
        sends.append(
            pltpu.make_async_remote_copy(
                src_ref=packet,
                dst_ref=packets.at[tile],
                send_sem=send_p.at[k],
                recv_sem=recv_p.at[k],
                device_id=(face, lax.rem(tile + k, tiles)),
                device_id_type=MESH,
            )
        )
        sends[-1].start()
    for copy in sends:
        copy.wait()
    for side, owner in ((0, 0), (1, tiles - 1)):

        @pl.when(tile == owner)
        def _():
            for k in range(1, tiles):
                end_copy(k, side).wait_send()

        @pl.when(tile != owner)
        def _():
            end_copy(1, side).wait_recv()

    per = 128 // nrow
    for side in range(2):
        line[side] = jnp.concatenate([ends[side, k] for k in range(4)], axis=1).astype(f32)
        parts = []
        for block in range(tiles // per):
            acc = jnp.zeros((chans, 128), f32)
            for i in range(per):
                seg = packets[block * per + i].astype(f32)
                seg = pltpu.roll(seg, (128 + (i - side) * nrow) % 128, 1) if i != side else seg
                acc = jnp.where((lane >= i * nrow) & (lane < (i + 1) * nrow), seg, acc)
            parts.append(acc)
        line[2 + side] = jnp.concatenate(parts, axis=1)
    width = tiles * nrow
    for s in range(4):
        full = line[s]
        for k in range(4):
            lots[s, k] = full[:, k * 128 : (k + 1) * 128].astype(bf16)
        near = pltpu.roll(full, lax.rem(width + 1 - tile * nrow, width), 1)[:, 0:128]
        far = pltpu.roll(full, lax.rem(width + 65 - (tiles - 1 - tile) * nrow, width), 1)[:, 0:128]
        wins[s] = jnp.where(lane < 64, near, far).astype(bf16)
    windows[face] = wins[...]
    sends = []
    for k in range(1, faces):
        sends.append(
            pltpu.make_async_remote_copy(
                src_ref=wins,
                dst_ref=windows.at[face],
                send_sem=send_n.at[k],
                recv_sem=recv_n.at[k],
                device_id=(lax.rem(face + k, faces), tile),
                device_id_type=MESH,
            )
        )
        sends[-1].start()

    def lot_copy(k):
        peer = lax.rem(face + k, faces)
        return pltpu.make_async_remote_copy(
            src_ref=chosen.at[k],
            dst_ref=whole.at[face],
            send_sem=send_l.at[k],
            recv_sem=recv_l.at[k],
            device_id=(peer, tile),
            device_id_type=MESH,
        )

    at_end = (tile == 0) | (tile == tiles - 1)
    end_side = jnp.where(tile == 0, 0, 1)

    @pl.when(at_end)
    def _():
        for k in range(1, faces):
            chosen[k] = lots[link_ref[lax.rem(face + k, faces), end_side, 1]]
            lot_copy(k).start()

    for copy in vertical:
        copy.wait()
    for copy in sends:
        copy.wait()
    for side in range(2):
        view = windows[link_ref[face, 2 + side, 0], link_ref[face, 2 + side, 1]]
        spot = jnp.where(link_ref[face, 2 + side, 2] == 1, 65 + nrow - col, col)
        turn = (row == spot).astype(bf16)
        cols_ref[side] = jnp.dot(view, turn, preferred_element_type=f32).astype(bf16)
        rows_ref[side] = (upper, lower)[side][...]

    @pl.when(at_end)
    def _():
        for k in range(1, faces):
            lot_copy(k).wait()

    for side, owner in ((0, 0), (1, tiles - 1)):

        @pl.when(tile == owner)
        def _():
            flip = link_ref[face, side, 2] == 1
            turn = (row == jnp.where(flip, 127 - col, col)).astype(bf16)
            for k in range(4):
                view = whole[link_ref[face, side, 0], jnp.where(flip, 3 - k, k)]
                rows_ref[side, k] = jnp.dot(view, turn, preferred_element_type=f32).astype(bf16)
    whole_box = pl.ds(0, count - 1)
    pltpu.make_async_copy(box.at[whole_box], got.at[whole_box], send_1).wait()
    pltpu.make_async_copy(box2.at[whole_box], got2.at[whole_box], send_2).wait()


def remap_call(pick, links, entries, nested, source, weight, collective_id):
    faces, tiles = lax.axis_size("face"), lax.axis_size("tile")
    count = faces * tiles
    dma = pltpu.SemaphoreType.DMA
    f32, bf16 = jnp.float32, jnp.bfloat16
    mem = pltpu.VMEM
    chans = source.shape[1]
    block = (4, chans, 128)
    return pl.pallas_call(
        functools.partial(remap_kernel, faces, tiles),
        out_shape=(
            jax.ShapeDtypeStruct((count, chans, 128), bf16),
            jax.ShapeDtypeStruct((2,) + block, bf16),
            jax.ShapeDtypeStruct((2, chans, 128), bf16),
        ),
        in_specs=[SM, SM, VM, VM, VM, pl.BlockSpec(memory_space=pltpu.HBM)],
        out_specs=(VM, VM, VM),
        scratch_shapes=[
            mem(weight.shape, bf16),
            mem((count, chans, 128), bf16),
            mem((count, 32, 128), bf16),
            mem((count, 32, 128), bf16),
            mem((faces, tiles, 2, 128), jnp.int32),
            mem((count, 128), jnp.int32),
            mem((count, 128), jnp.int32),
            mem((count * 40 + 40, 128), f32),
            mem((count * 24 + 24, 128), f32),
            mem((count, chans, 128), bf16),
            mem((count, chans, 128), bf16),
            mem((2,) + block, bf16),
            mem(block, bf16),
            mem(block, bf16),
            mem((chans, 128), bf16),
            mem((tiles, chans, 128), bf16),
            mem((2,) + block, bf16),
            mem((4, chans, 512), f32),
            mem(block, bf16),
            mem((4,) + block, bf16),
            mem((faces,) + block, bf16),
            mem((faces,) + block, bf16),
            mem((faces,) + block, bf16),
            mem((2, 128), jnp.int32),
            mem((8, 128), jnp.int32),
            pltpu.SMEM((8, 128), jnp.int32),
            dma((4,)),
            dma, dma, dma, dma, dma, dma,
            dma((tiles,)), dma((tiles,)), dma((faces,)), dma((faces,)),
            dma((2,)), dma((2,)), dma((tiles,)), dma((tiles,)), dma((tiles,)), dma((2,)), dma((faces,)), dma((faces,)),
            dma((faces,)), dma((faces,)),
        ],
        compiler_params=pltpu.CompilerParams(
            collective_id=collective_id, has_side_effects=True, vmem_limit_bytes=VMEM_BYTES
        ),
    )(pick, links, entries, nested, source, weight)


def reduce_kernel(
    faces, tiles, wide_ref, one_ref, two_ref, ker_ref, grad_ref, first, part, second, mine, full, send_a, recv_a, send_b, recv_b,
    send_c, recv_c,
):
    face = lax.axis_index("face")
    tile = lax.axis_index("tile")
    f32, bf16 = jnp.float32, jnp.bfloat16
    size = wide_ref.shape[0] // tiles
    barrier = pltpu.get_barrier_semaphore()
    for k in range(1, tiles):
        pl.semaphore_signal(barrier, inc=1, device_id=(face, lax.rem(tile + k, tiles)), device_id_type=MESH)
    for k in range(1, faces):
        pl.semaphore_signal(barrier, inc=1, device_id=(lax.rem(face + k, faces), tile), device_id_type=MESH)
    grad_ref[...] = wide_ref[...].astype(bf16)
    pl.semaphore_wait(barrier, tiles + faces - 2)

    def spot(t):
        return pl.ds(pl.multiple_of(t * size, 16), size)

    copies = []
    for k in range(1, tiles):
        peer = lax.rem(tile + k, tiles)
        copies.append(
            pltpu.make_async_remote_copy(
                src_ref=grad_ref.at[spot(peer)],
                dst_ref=first.at[k],
                send_sem=send_a.at[k],
                recv_sem=recv_a.at[k],
                device_id=(face, peer),
                device_id_type=MESH,
            )
        )
        copies[-1].start()
    total = wide_ref[spot(tile), :]
    for k in range(1, tiles):
        copies[k - 1].wait_recv()
        total = total + first[k].astype(f32)
    part[...] = total.astype(bf16)
    second[face] = part[...]
    later = []
    for k in range(1, faces):
        later.append(
            pltpu.make_async_remote_copy(
                src_ref=part,
                dst_ref=second.at[face],
                send_sem=send_b.at[k],
                recv_sem=recv_b.at[k],
                device_id=(lax.rem(face + k, faces), tile),
                device_id_type=MESH,
            )
        )
        later[-1].start()
    for copy in later:
        copy.wait_recv()
    total = second[0].astype(f32)
    for k in range(1, faces):
        total = total + second[k].astype(f32)
    mine[...] = total.astype(bf16)
    full[spot(tile), :] = mine[...]
    last = []
    for k in range(1, tiles):
        last.append(
            pltpu.make_async_remote_copy(
                src_ref=mine,
                dst_ref=full.at[spot(tile)],
                send_sem=send_c.at[k],
                recv_sem=recv_c.at[k],
                device_id=(face, lax.rem(tile + k, tiles)),
                device_id_type=MESH,
            )
        )
        last[-1].start()
    for copy in last:
        copy.wait_recv()
    two_ref[...] = full[0:384, :].astype(f32).T[0:90, 0:360]
    one_ref[...] = full[384:768, :].astype(f32).T[0:90, 0:360]
    ker_ref[...] = full[368:384, 0:90].astype(f32)[0:9]
    for copy in copies + later + last:
        copy.wait_send()


def reduce_call(grad, collective_id):
    faces, tiles = lax.axis_size("face"), lax.axis_size("tile")
    dma = pltpu.SemaphoreType.DMA
    f32, bf16 = jnp.float32, jnp.bfloat16
    size = grad.shape[0] // tiles
    return pl.pallas_call(
        functools.partial(reduce_kernel, faces, tiles),
        out_shape=(
            jax.ShapeDtypeStruct((90, 360), f32),
            jax.ShapeDtypeStruct((90, 360), f32),
            jax.ShapeDtypeStruct((9, 90), f32),
        ),
        in_specs=[VM],
        out_specs=(VM, VM, VM),
        scratch_shapes=[
            pltpu.VMEM(grad.shape, bf16),
            pltpu.VMEM((tiles, size, 128), bf16),
            pltpu.VMEM((size, 128), bf16),
            pltpu.VMEM((faces, size, 128), bf16),
            pltpu.VMEM((size, 128), bf16),
            pltpu.VMEM(grad.shape, bf16),
            dma((tiles,)), dma((tiles,)), dma((faces,)), dma((faces,)), dma((tiles,)), dma((tiles,)),
        ],
        compiler_params=pltpu.CompilerParams(
            collective_id=collective_id, has_side_effects=True, vmem_limit_bytes=24 * MIB
        ),
    )(grad)


def remap(source, entry_block, entry_source, entry_weight, lat_to_nested, face_links):
    return remap_call(entry_source, face_links, entry_block[None], lat_to_nested[None], source, entry_weight, 1)

def per_device(
    source, entry_block, entry_source, entry_weight, lat_to_nested, face_links, w_in, b_in, kernel, ln_gain, ln_bias,
    w_one, b_one, w_two, b_two, cotangent,
):
    face_count = lax.axis_size("face")
    width = cotangent.shape[3]
    box, rows, cols = remap(source, entry_block, entry_source, entry_weight, lat_to_nested, face_links)
    scale = 1.0 / math.sqrt(face_count * width * width)
    output, grad = strip_call(
        box, rows, cols, cotangent[0], w_in, b_in, kernel, ln_gain, ln_bias, w_one, b_one, w_two, b_two,
        scale,
    )
    grad_one, grad_two, grad_kernel = reduce_call(grad, 4)
    return (output[None], grad_one, grad_two.T, grad_kernel)


def solution(mesh):
    split = P(("face", "tile"))
    strips = P("face", None, "tile", None)
    return jax.shard_map(
        per_device,
        mesh=mesh,
        in_specs=(split,) * 5 + (P(),) * 10 + (strips,),
        out_specs=(strips, P(), P(), P()),
        check_vma=False,
    )
```

```python
import functools
import math

import jax
import jax.numpy as jnp
from jax import lax
from jax.experimental import pallas as pl
from jax.experimental.pallas import tpu as pltpu
from jax.sharding import PartitionSpec as P


GELU_K = 0.7978845608028654
GELU_C = 0.044715
NORM_EPS = 1e-06
CP = 96
HP = 368
PITCH = 40
SLOTS = 4
MIB = 1024 * 1024


def strip_kernel(
    blocks_ref, rows_ref, cols_ref, cot_ref, win_ref, bin_ref, ker_ref, gain_ref, bias_ref, wone_ref,
    bone_ref, wtwo_ref, btwo_ref, out_ref, grad_ref, cot_v, out_v, field, cols, depth, back_d, turn_s, cot_t, out_t,
    scaled_s, norm_s, stds_s, pre_s, back_s, hid_s, bp_s, raw_s, g2_s, g1_s, gk_s, tab_s, vec_s, flat_s, w_in_s, w1t_s,
    w1_s, w2t_s, w2_s, sem_in, sem_out, scale,
):
    chans, rows, width = cot_ref.shape
    hidden = wone_ref.shape[1]
    lanes = width // 128
    f32, bf16 = jnp.float32, jnp.bfloat16
    nt = (((1,), (1,)), ((), ()))

    def wide(v):
        return jnp.concatenate([v] * lanes, axis=1)

    bring = pltpu.make_async_copy(cot_ref, cot_v, sem_in)
    bring.start()

    tab_s[...] = jnp.zeros_like(tab_s)
    for j, ref in enumerate((bin_ref, gain_ref, bias_ref, btwo_ref)):
        tab_s[j : j + 1, 0:chans] = ref[...]
    tab_s[4:13, 0:chans] = ker_ref[...]
    turned = tab_s[...].T
    for j in range(13):
        vec_s[j] = jnp.broadcast_to(turned[0:CP, j : j + 1], (CP, 128))
    tab_s[...] = jnp.zeros_like(tab_s)
    tab_s[0:16, 0:chans] = win_ref[...].astype(f32)
    w_in_s[...] = tab_s[...].T[0:CP, 0:16].astype(bf16)
    flat_s[...] = jnp.zeros_like(flat_s)
    flat_s[0:chans, 0:hidden] = wone_ref[...].astype(f32)
    w1_s[...] = flat_s[0:CP, 0:HP].astype(bf16)
    bone = bone_ref[0:1, 0:hidden]
    high = bone.astype(bf16).astype(f32)
    flat_s[chans : chans + 1, 0:hidden] = high
    flat_s[chans + 1 : chans + 2, 0:hidden] = bone - high
    w1t_s[...] = (flat_s[...].T[0:HP, 0:CP] * 0.5).astype(bf16)
    flat_s[...] = jnp.zeros_like(flat_s)
    flat_s[0:chans, 0:hidden] = wtwo_ref[...].astype(f32)
    w2t_s[...] = flat_s[0:CP, 0:HP].astype(bf16)
    w2_s[...] = (flat_s[...].T[0:HP, 0:CP] * 0.5).astype(bf16)

    tile, tile_count = lax.axis_index("tile"), lax.axis_size("tile")
    lane = lax.broadcasted_iota(jnp.int32, (CP, 128), 1)
    last = lane == jnp.where(tile == tile_count - 1, rows + 1, -1)
    first = lane == jnp.where(tile == 0, 0, -1)
    for side in range(2):
        v = jnp.dot(w_in_s[...], cols_ref[side], preferred_element_type=f32) + vec_s[0]
        cols[side] = jnp.where(first | last, 0.0, v.astype(bf16).astype(f32))

    g2_s[...] = jnp.zeros_like(g2_s)
    g1_s[...] = jnp.zeros_like(g1_s)
    def make_row(at, x):
        lat = jnp.dot(w_in_s[...], x, preferred_element_type=f32) + wide(vec_s[0])
        lat = lat.astype(bf16).astype(f32)
        wide_lane = lax.broadcasted_iota(jnp.int32, (CP, 128), 1)
        mid = [lat[:, k * 128 : (k + 1) * 128] for k in range(lanes)]
        up = [pltpu.roll(cols[0], lax.rem(128 - at, 128), 1)] + [pltpu.roll(m, 1, 1) for m in mid]
        dn = [pltpu.roll(m, 127, 1) for m in mid] + [pltpu.roll(cols[1], 127 - at, 1)]
        for k in range(lanes):
            part = slice(k * 128, (k + 1) * 128)
            field[at, 0, :, part] = jnp.where(wide_lane == 0, up[k], up[k + 1])
            field[at, 1, :, part] = mid[k]
            field[at, 2, :, part] = jnp.where(wide_lane == 127, dn[k + 1], dn[k])

    make_row(0, jnp.concatenate([rows_ref[0, k] for k in range(lanes)], axis=1))
    make_row(rows + 1, jnp.concatenate([rows_ref[1, k] for k in range(lanes)], axis=1))

    def row_step(r, _):
        make_row(r + 1, jnp.concatenate([blocks_ref[r * lanes + k] for k in range(lanes)], axis=1))
        return 0

    lax.fori_loop(0, rows, row_step, 0, unroll=2)

    bring.wait()
    turn_s[...] = jnp.zeros_like(turn_s)

    def turn(i, _):
        for j in range(16):
            c = i * 16 + j

            @pl.when(c < chans)
            def _():
                x = cot_v[c].astype(f32)
                for k in range(lanes):
                    turn_s[k, j * PITCH : j * PITCH + rows, :] = x[:, k * 128 : (k + 1) * 128]

        for r in range(rows):
            x = jnp.concatenate([turn_s[k, pl.ds(r, 16, stride=PITCH), :] for k in range(lanes)], axis=1)
            cot_t[r, pl.ds(pl.multiple_of(i * 16, 16), 16), :] = x.astype(bf16)
        return 0

    lax.fori_loop(0, CP // 16, turn, 0)

    def shifted(r, c):
        return [
            [field[r, side, pl.ds(c, 8), k * 128 : (k + 1) * 128] for k in range(lanes)] for side in range(3)
        ]

    def conv_chunk(i, _):
        c = pl.multiple_of(i * 8, 8)
        w = [vec_s[4 + tap, pl.ds(c, 8), :] for tap in range(9)]

        def mix(a, views, k):
            return w[3 * a] * views[0][k] + w[3 * a + 1] * views[1][k] + w[3 * a + 2] * views[2][k]

        v0, v1 = shifted(0, c), shifted(1, c)
        one = tuple(mix(0, v0, k) + mix(1, v1, k) for k in range(lanes))
        two = tuple(mix(0, v1, k) for k in range(lanes))

        def go(r, carry):
            one, two = carry
            v = shifted(r + 2, c)
            for k in range(lanes):
                depth[r, pl.ds(c, 8), k * 128 : (k + 1) * 128] = one[k] + mix(2, v, k)
            return (
                tuple(two[k] + mix(1, v, k) for k in range(lanes)),
                tuple(mix(0, v, k) for k in range(lanes)),
            )

        lax.fori_loop(0, rows, go, (one, two), unroll=4)
        return 0

    lax.fori_loop(0, CP // 8, conv_chunk, 0)

    row_id = lax.broadcasted_iota(jnp.int32, (CP, 128), 0)
    real = row_id < chans
    ones_rows = (row_id == chans) | (row_id == chans + 1)

    def col_sum(v):
        return jnp.sum(v, axis=0, keepdims=True)

    def norm_units(r, u):
        def unit(k):
            part = slice(k * 128, (k + 1) * 128)
            d = depth[r, :, part]
            d = d - col_sum(d) * (1.0 / chans)
            d = jnp.where(real, d, 0.0)
            inv_std = lax.rsqrt(col_sum(d * d) * (1.0 / chans) + NORM_EPS)
            s = d * inv_std
            at = lax.rem(r, 8)
            scaled_s[at, :, part] = s
            stds_s[at, :, part] = jnp.broadcast_to(inv_std, (8, 128))
            n = jnp.where(ones_rows, 1.0, s * vec_s[1] + vec_s[2])
            norm_s[u % 4, :, part] = n.astype(bf16)

        return [functools.partial(unit, k) for k in range(lanes)]

    halves = [slice(n, n + 256) for n in range(0, width, 256)]

    def widen_units(r, u):
        def pre(part):
            x = jnp.dot(w1t_s[...], norm_s[u % 4, :, part], preferred_element_type=f32)
            pre_s[u % 2, :, part] = x.astype(bf16)

        def back(part):
            x = jnp.dot(w2_s[...], cot_t[r, :, part], preferred_element_type=f32)
            back_s[u % 2, :, part] = x.astype(bf16)

        return [functools.partial(f, part) for part in halves for f in (pre, back)]

    def gelu_units(r, u):
        num = lambda v: jnp.asarray(v, bf16)

        def unit(h):
            x = pre_s[u % 2, h : h + 16, :]
            q = x * x
            t = jnp.tanh(x * (num(2.0 * GELU_K) + num(8.0 * GELU_K * GELU_C) * q))
            p = num(1.0) + t
            g = x * p
            slope = p + g * (num(1.0) - t) * (num(2.0 * GELU_K) + num(24.0 * GELU_K * GELU_C) * q)
            hid_s[u % 2, h : h + 16, :] = g
            bp_s[u % 2, h : h + 16, :] = back_s[u % 2, h : h + 16, :] * slope

        return [functools.partial(unit, h) for h in range(0, HP, 16)]

    def narrow_units(r, u):
        def out(part):
            raw_s[u % 2, 0, :, part] = jnp.dot(w2t_s[...], hid_s[u % 2, :, part], preferred_element_type=f32)

        def hat(part):
            raw_s[u % 2, 1, :, part] = jnp.dot(w1_s[...], bp_s[u % 2, :, part], preferred_element_type=f32)

        def two():
            g2_s[...] += lax.dot_general(hid_s[u % 2], cot_t[r], nt, preferred_element_type=f32)

        def one():
            g1_s[...] += lax.dot_general(bp_s[u % 2], norm_s[u % 4], nt, preferred_element_type=f32)

        units = [functools.partial(f, part) for part in halves for f in (out, hat)]
        return [units[0], units[1], two, units[2], units[3], one]

    def rear_units(r, u):
        def unit(k):
            part = slice(k * 128, (k + 1) * 128)
            at = lax.rem(r, 8)
            out_t[r, :, part] = (raw_s[u % 2, 0, :, part] + vec_s[3] + field[r + 1, 1, :, part]).astype(bf16)
            inv_std = stds_s[at, 0:1, part]
            b = raw_s[u % 2, 1, :, part] * vec_s[1]
            s = scaled_s[at, :, part]
            one = col_sum(b) * (inv_std * (1.0 / chans))
            two = col_sum(b * s) * (inv_std * (1.0 / chans))
            back_d[r, :, part] = b * inv_std - one - s * two

        return [functools.partial(unit, k) for k in range(lanes)]

    def beat(at, u, live):
        units = [
            make(at - s, u - s) if ok else []
            for s, (make, ok) in enumerate(zip((norm_units, widen_units, gelu_units, narrow_units, rear_units), live))
        ]
        vector = units[2]
        extra = units[0] + units[4]
        if extra and vector:
            gap = max(1, len(vector) // len(extra))
            mixed = []
            for i, v in enumerate(vector):
                mixed.append(v)
                if i % gap == gap - 1 and extra:
                    mixed.append(extra.pop(0))
            vector = mixed + extra
        else:
            vector = vector + extra
        matrix = []
        for i in range(max(len(units[1]), len(units[3]))):
            matrix += units[3][i : i + 1] + units[1][i : i + 1]
        share = len(vector) / max(1, len(matrix))
        done = 0
        for i, m in enumerate(matrix):
            m()
            upto = round((i + 1) * share)
            for v in vector[done:upto]:
                v()
            done = upto
        for v in vector[done:]:
            v()

    for at in range(4):
        beat(at, at, [at - s >= 0 for s in range(5)])

    def step(i, _):
        for u in range(SLOTS):
            beat(4 + i * SLOTS + u, 4 + u, [True] * 5)
        return 0

    lax.fori_loop(0, rows // SLOTS - 1, step, 0)
    for at in range(rows, rows + 4):
        beat(at, at, [at - s < rows for s in range(5)])

    def back(i, _):
        for r in range(rows):
            x = out_t[r, pl.ds(pl.multiple_of(i * 16, 16), 16), :].astype(f32)
            for k in range(lanes):
                turn_s[k, pl.ds(r, 16, stride=PITCH), :] = x[:, k * 128 : (k + 1) * 128]
        for j in range(16):
            c = i * 16 + j

            @pl.when(c < chans)
            def _():
                x = jnp.concatenate([turn_s[k, j * PITCH : j * PITCH + rows, :] for k in range(lanes)], axis=1)
                out_v[c] = x.astype(bf16)

        return 0

    lax.fori_loop(0, CP // 16, back, 0)
    take = pltpu.make_async_copy(out_v, out_ref, sem_out)
    take.start()

    def kernel_chunk(i, _):
        c = pl.multiple_of(i * 8, 8)

        def grad_row(r):
            return tuple(back_d[r, pl.ds(c, 8), k * 128 : (k + 1) * 128] for k in range(lanes))

        def fold(acc, a, b, views):
            new = list(acc)
            for s in range(3):
                m = b[0] * views[s][0]
                for k in range(1, lanes):
                    m = m + b[k] * views[s][k]
                new[3 * a + s] = new[3 * a + s] + m
            return tuple(new)

        acc = tuple(jnp.zeros((8, 128), f32) for _ in range(9))
        b0 = grad_row(0)
        acc = fold(acc, 0, b0, shifted(0, c))
        b1 = grad_row(1)
        v = shifted(1, c)
        acc = fold(fold(acc, 0, b1, v), 1, b0, v)

        def go(r, carry):
            acc, b1, b0 = carry
            v = shifted(r, c)
            b = grad_row(r)
            acc = fold(fold(fold(acc, 0, b, v), 1, b1, v), 2, b0, v)
            return acc, b, b1

        acc, b1, b0 = lax.fori_loop(2, rows, go, (acc, b1, b0), unroll=3)
        v = shifted(rows, c)
        acc = fold(fold(acc, 1, b1, v), 2, b0, v)
        acc = fold(acc, 2, b1, shifted(rows + 1, c))
        for tap in range(9):
            gk_s[tap, pl.ds(c, 8), :] = acc[tap]
        return 0

    lax.fori_loop(0, CP // 8, kernel_chunk, 0)
    grad_ref[360:384, :] = jnp.zeros((24, 128), f32)
    grad_ref[744:768, :] = jnp.zeros((24, 128), f32)
    grad_ref[0:hidden, 0:CP] = g2_s[0:hidden, :] * scale
    grad_ref[384 : 384 + hidden, 0:CP] = g1_s[0:hidden, :] * scale
    ones = jnp.ones((8, 128), f32)
    for tap in range(9):
        line = lax.dot_general(ones, gk_s[tap], nt, preferred_element_type=f32, precision=lax.Precision.HIGHEST)
        grad_ref[368 + tap : 369 + tap, 0:CP] = line[0:1, :] * scale
    take.wait()


def strip_call(blocks, rows, cols, cot, w_in, b_in, kernel, ln_gain, ln_bias, w_one, b_one, w_two, b_two, scale):
    chans, nrow, width = cot.shape
    f32, bf16 = jnp.float32, jnp.bfloat16
    lanes = width // 128
    vm = pl.BlockSpec(memory_space=pltpu.VMEM)
    hbm = pl.BlockSpec(memory_space=pltpu.HBM)
    mem = pltpu.VMEM
    return pl.pallas_call(
        functools.partial(strip_kernel, scale=scale),
        out_shape=(jax.ShapeDtypeStruct((chans, nrow, width), bf16), jax.ShapeDtypeStruct((768, 128), f32)),
        in_specs=[vm] * 3 + [hbm] + [vm] * 9,
        out_specs=(hbm, vm),
        scratch_shapes=[
            mem((chans, nrow, width), bf16),
            mem((chans, nrow, width), bf16),
            mem((nrow + 2, 3, CP, width), f32),
            mem((2, CP, 128), f32),
            mem((nrow, CP, width), f32),
            mem((nrow, CP, width), f32),
            mem((lanes, 17 * PITCH, 128), f32),
            mem((nrow, CP, width), bf16),
            mem((nrow, CP, width), bf16),
            mem((8, CP, width), f32),
            mem((4, CP, width), bf16),
            mem((8, 8, width), f32),
            mem((2, HP, width), bf16),
            mem((2, HP, width), bf16),
            mem((2, HP, width), bf16),
            mem((2, HP, width), bf16),
            mem((2, 2, CP, width), f32),
            mem((HP, CP), f32),
            mem((HP, CP), f32),
            mem((9, CP, 128), f32),
            mem((16, 128), f32),
            mem((13, CP, 128), f32),
            mem((128, 384), f32),
            mem((CP, 16), bf16),
            mem((HP, CP), bf16),
            mem((CP, HP), bf16),
            mem((CP, HP), bf16),
            mem((HP, CP), bf16),
            pltpu.SemaphoreType.DMA,
            pltpu.SemaphoreType.DMA,
        ],
        compiler_params=pltpu.CompilerParams(vmem_limit_bytes=60 * MIB),
    )(
        blocks, rows, cols, cot, w_in, b_in[None], kernel, ln_gain[None], ln_bias[None], w_one, jnp.pad(b_one, (0, 512 - b_one.shape[0]))[None],
        w_two.T, b_two[None],
    )


MESH = pl.DeviceIdType.MESH
MIB = 1024 * 1024
VMEM_BYTES = 60 * MIB
VM = pl.BlockSpec(memory_space=pltpu.VMEM)
SM = pl.BlockSpec(memory_space=pltpu.SMEM)
AXES = ("face", "tile")


def remap_kernel(
    faces, tiles, pick_ref, link_ref, entry_ref, nested_ref, source_ref, weight_ref, placed_ref, rows_ref, cols_ref, weight,
    part, box, got, table, block_of, nest_of, wide_s, narrow_s, box2, got2, edge, upper, lower, packet, packets, ends,
    line, wins, lots, chosen, windows, whole, ids, slot_v, slot_s, send_w, send_s, send_1, recv_1, local, send_2, recv_2, send_ia, recv_ia, send_ib, recv_ib,
    send_v, recv_v, send_p, recv_p, send_e, recv_e, send_n, recv_n, send_l, recv_l,
):
    f32, bf16 = jnp.float32, jnp.bfloat16
    face = lax.axis_index("face")
    tile = lax.axis_index("tile")
    count = faces * tiles
    me = face * tiles + tile
    chans = source_ref.shape[1]
    nrow = count // 4
    loads = weight_ref.shape[0] // 4

    def load(k):
        span = pl.ds(k * loads, loads)
        return pltpu.make_async_copy(weight_ref.at[span], weight.at[span], send_w.at[k])

    for k in range(4):
        load(k).start()
    barrier = pltpu.get_barrier_semaphore()

    def greet(k, _):
        peer = lax.rem(me + k, count)
        pl.semaphore_signal(barrier, inc=1, device_id=(peer // tiles, lax.rem(peer, tiles)), device_id_type=MESH)
        return 0

    lax.fori_loop(1, count, greet, 0)

    row = lax.broadcasted_iota(jnp.int32, (count, count), 0)
    col = lax.broadcasted_iota(jnp.int32, (count, count), 1)

    def turned(v):
        return jnp.broadcast_to(v, (count, count)).T

    ids[0:1, :] = entry_ref[...]
    ids[1:2, :] = nested_ref[...]
    hit = (jnp.broadcast_to(entry_ref[...], (count, count)) >> 7) == row
    fcol = col.astype(f32)
    low = turned(jnp.min(jnp.where(hit, fcol, float(count - 1)), axis=1, keepdims=True))
    high = turned(jnp.max(jnp.where(hit, fcol, 0.0), axis=1, keepdims=True))
    slot_v[...] = jnp.where(row[0:8] == 0, low[0:8], high[0:8]).astype(jnp.int32)
    to_scalars = pltpu.make_async_copy(slot_v, slot_s, send_s)
    to_scalars.start()

    group = 8
    for k in range(4):
        load(k).wait()

        def multiply(i, _):
            for j in range(group):
                e = k * loads + i * group + j
                x = jnp.dot(source_ref[pick_ref[e]], weight[e], preferred_element_type=f32)
                part[e] = x.astype(bf16)
            return 0

        lax.fori_loop(0, loads // group, multiply, 0)

    to_scalars.wait()

    def fill(d, _):
        box[d, 0:16, :] = part[slot_s[0, d] & (count - 1)]
        box[d, 16:32, :] = part[slot_s[1, d] & (count - 1)]
        return 0

    lax.fori_loop(0, count, fill, 0, unroll=8)
    table[face, tile] = ids[...]
    pl.semaphore_wait(barrier, count - 1)

    index = []
    for k in range(1, tiles):
        index.append(
            pltpu.make_async_remote_copy(
                src_ref=ids,
                dst_ref=table.at[face, tile],
                send_sem=send_ia.at[k],
                recv_sem=recv_ia.at[k],
                device_id=(face, lax.rem(tile + k, tiles)),
                device_id_type=MESH,
            )
        )
        index[-1].start()

    def exchange(src, dst, send, recv):
        def push(k, _):
            peer = lax.rem(me + k, count)
            pltpu.make_async_remote_copy(
                src_ref=src.at[peer],
                dst_ref=dst.at[me],
                send_sem=send,
                recv_sem=recv,
                device_id=(peer // tiles, lax.rem(peer, tiles)),
                device_id_type=MESH,
            ).start()
            return 0

        lax.fori_loop(1, count, push, 0, unroll=2)
        own = pltpu.make_async_copy(src.at[me], dst.at[me], local)
        own.start()
        return own

    def arrive(own, src, dst, recv):
        whole_box = pl.ds(0, count - 1)
        own.wait()
        pltpu.make_async_copy(src.at[whole_box], dst.at[whole_box], recv).wait()

    own = exchange(box, got, send_1, recv_1)
    for copy in index:
        copy.wait()
    index = []
    for k in range(1, faces):
        index.append(
            pltpu.make_async_remote_copy(
                src_ref=table.at[face],
                dst_ref=table.at[face],
                send_sem=send_ib.at[k],
                recv_sem=recv_ib.at[k],
                device_id=(lax.rem(face + k, faces), tile),
                device_id_type=MESH,
            )
        )
        index[-1].start()
    for copy in index:
        copy.wait()

    def spread(f, _):
        for t in range(tiles):
            pair = table[f, t]
            block_of[pl.ds(f * tiles + t, 1), :] = pair[0:1, :]
            nest_of[pl.ds(f * tiles + t, 1), :] = pair[1:2, :]
        return 0

    lax.fori_loop(0, faces, spread, 0)
    blocks = block_of[...]
    hit = (blocks >> 7) == me
    key = (col * count + (blocks & (count - 1))).astype(f32)
    low = jnp.min(jnp.where(hit, key, 1e9), axis=1, keepdims=True)
    high = jnp.max(jnp.where(hit, key, -1.0), axis=1, keepdims=True)
    low_label = jnp.where(high >= 0.0, low.astype(jnp.int32) & (count - 1), -1).astype(f32)
    high_label = jnp.where(high > low, high.astype(jnp.int32) & (count - 1), -1).astype(f32)
    nest = jnp.broadcast_to(nested_ref[...], (count, count))
    perm = jnp.sum(jnp.where((nest >> 7) == row, col.astype(f32), 0.0), axis=1, keepdims=True)
    take_low = (turned(low_label) == perm).astype(f32).astype(bf16)
    take_high = (turned(high_label) == perm).astype(f32).astype(bf16)
    nest = nest_of[...]
    spot = jnp.sum(jnp.where((nest >> 7) == me, (nest & (count - 1)).astype(f32), 0.0), axis=1, keepdims=True)
    place = (turned(spot) == row.astype(f32)).astype(f32).astype(bf16)

    arrive(own, box, got, recv_1)
    deep = 40

    def widen(s, _):
        wide_s[pl.ds(pl.multiple_of(s * deep, 8), 32), :] = got[s].astype(f32)
        return 0

    lax.fori_loop(0, count, widen, 0, unroll=8)
    pitch = 24
    for c in range(chans):
        one = wide_s[pl.ds(c, count, stride=deep), :].astype(bf16)
        two = wide_s[pl.ds(16 + c, count, stride=deep), :].astype(bf16)
        y = jnp.dot(take_low, one, preferred_element_type=f32) + jnp.dot(take_high, two, preferred_element_type=f32)
        narrow_s[pl.ds(c, count, stride=pitch), :] = y

    def narrow(d, _):
        box2[d] = narrow_s[pl.ds(pl.multiple_of(d * pitch, 8), 16), :].astype(bf16)
        return 0

    lax.fori_loop(0, count, narrow, 0, unroll=8)
    own = exchange(box2, got2, send_2, recv_2)
    arrive(own, box2, got2, recv_2)

    def widen_two(s, _):
        wide_s[pl.ds(pl.multiple_of(s * pitch, 8), 16), :] = got2[s].astype(f32)
        return 0

    lax.fori_loop(0, count, widen_two, 0, unroll=8)
    for c in range(chans):
        one = wide_s[pl.ds(c, count, stride=pitch), :].astype(bf16)
        narrow_s[pl.ds(c, count, stride=pitch), :] = jnp.dot(place, one, preferred_element_type=f32)

    def settle(m, _):
        placed_ref[m] = narrow_s[pl.ds(pl.multiple_of(m * pitch, 8), 16), :].astype(bf16)
        return 0

    lax.fori_loop(0, count, settle, 0, unroll=8)

    for k in range(4):
        edge[0, k] = placed_ref[k]
        edge[1, k] = placed_ref[4 * nrow - 4 + k]
    down = lax.rem(tile + 1, tiles)
    up = lax.rem(tile + tiles - 1, tiles)
    vertical = []
    for k, (dst, peer) in enumerate(((upper, down), (lower, up))):
        vertical.append(
            pltpu.make_async_remote_copy(
                src_ref=edge.at[1 - k],
                dst_ref=dst,
                send_sem=send_v.at[k],
                recv_sem=recv_v.at[k],
                device_id=(face, peer),
                device_id_type=MESH,
            )
        )
        vertical[-1].start()

    lane = lax.broadcasted_iota(jnp.int32, (chans, 128), 1)

    def pick(r, acc):
        left = pltpu.roll(placed_ref[4 * r].astype(f32), r, 1)
        right = pltpu.roll(placed_ref[4 * r + 3].astype(f32), r + nrow + 1, 1)
        return jnp.where(lane == r, left, jnp.where(lane == r + nrow, right, acc))

    packet[...] = lax.fori_loop(0, nrow, pick, jnp.zeros((chans, 128), f32), unroll=8).astype(bf16)
    packets[tile] = packet[...]
    sends = []
    for k in range(1, tiles):
        sends.append(
            pltpu.make_async_remote_copy(
                src_ref=packet,
                dst_ref=packets.at[tile],
                send_sem=send_p.at[k],
                recv_sem=recv_p.at[k],
                device_id=(face, lax.rem(tile + k, tiles)),
                device_id_type=MESH,
            )
        )
        sends[-1].start()
    def end_copy(k, side):
        return pltpu.make_async_remote_copy(
            src_ref=edge.at[side],
            dst_ref=ends.at[side],
            send_sem=send_e.at[k],
            recv_sem=recv_e.at[side],
            device_id=(face, lax.rem(tile + k, tiles)),
            device_id_type=MESH,
        )

    for side, owner in ((0, 0), (1, tiles - 1)):

        @pl.when(tile == owner)
        def _():
            for k in range(1, tiles):
                end_copy(k, side).start()
            ends[side] = edge[side]

    for copy in sends:
        copy.wait()
    for side, owner in ((0, 0), (1, tiles - 1)):

        @pl.when(tile == owner)
        def _():
            for k in range(1, tiles):
                end_copy(k, side).wait_send()

        @pl.when(tile != owner)
        def _():
            end_copy(1, side).wait_recv()

    per = 128 // nrow
    for side in range(2):
        line[side] = jnp.concatenate([ends[side, k] for k in range(4)], axis=1).astype(f32)
        parts = []
        for block in range(tiles // per):
            acc = jnp.zeros((chans, 128), f32)
            for i in range(per):
                seg = packets[block * per + i].astype(f32)
                seg = pltpu.roll(seg, (128 + (i - side) * nrow) % 128, 1) if i != side else seg
                acc = jnp.where((lane >= i * nrow) & (lane < (i + 1) * nrow), seg, acc)
            parts.append(acc)
        line[2 + side] = jnp.concatenate(parts, axis=1)
    width = tiles * nrow
    for s in range(4):
        full = line[s]
        near = pltpu.roll(full, lax.rem(width + 1 - tile * nrow, width), 1)[:, 0:128]
        far = pltpu.roll(full, lax.rem(width + 65 - (tiles - 1 - tile) * nrow, width), 1)[:, 0:128]
        wins[s] = jnp.where(lane < 64, near, far).astype(bf16)
    windows[face] = wins[...]
    sends = []
    for k in range(1, faces):
        sends.append(
            pltpu.make_async_remote_copy(
                src_ref=wins,
                dst_ref=windows.at[face],
                send_sem=send_n.at[k],
                recv_sem=recv_n.at[k],
                device_id=(lax.rem(face + k, faces), tile),
                device_id_type=MESH,
            )
        )
        sends[-1].start()

    def lot_copy(k):
        peer = lax.rem(face + k, faces)
        return pltpu.make_async_remote_copy(
            src_ref=chosen.at[k],
            dst_ref=whole.at[face],
            send_sem=send_l.at[k],
            recv_sem=recv_l.at[k],
            device_id=(peer, tile),
            device_id_type=MESH,
        )

    at_end = (tile == 0) | (tile == tiles - 1)
    end_side = jnp.where(tile == 0, 0, 1)

    @pl.when(at_end)
    def _():
        for s in range(4):
            for k in range(4):
                lots[s, k] = line[s, :, k * 128 : (k + 1) * 128].astype(bf16)
        for k in range(1, faces):
            chosen[k] = lots[link_ref[1, end_side, lax.rem(face + k, faces)]]
            lot_copy(k).start()

    for copy in vertical:
        copy.wait()
    for copy in sends:
        copy.wait()
    for side in range(2):
        view = windows[link_ref[0, 2 + side, face], link_ref[1, 2 + side, face]]
        spot = jnp.where(link_ref[2, 2 + side, face] == 1, 65 + nrow - col, col)
        turn = (row == spot).astype(bf16)
        cols_ref[side] = jnp.dot(view, turn, preferred_element_type=f32).astype(bf16)
        rows_ref[side] = (upper, lower)[side][...]

    @pl.when(at_end)
    def _():
        for k in range(1, faces):
            lot_copy(k).wait()

    for side, owner in ((0, 0), (1, tiles - 1)):

        @pl.when(tile == owner)
        def _():
            flip = link_ref[2, side, face] == 1
            turn = (row == jnp.where(flip, 127 - col, col)).astype(bf16)
            for k in range(4):
                view = whole[link_ref[0, side, face], jnp.where(flip, 3 - k, k)]
                rows_ref[side, k] = jnp.dot(view, turn, preferred_element_type=f32).astype(bf16)
    whole_box = pl.ds(0, count - 1)
    pltpu.make_async_copy(box.at[whole_box], got.at[whole_box], send_1).wait()
    pltpu.make_async_copy(box2.at[whole_box], got2.at[whole_box], send_2).wait()


def remap_call(pick, links, entries, nested, source, weight, collective_id):
    faces, tiles = lax.axis_size("face"), lax.axis_size("tile")
    count = faces * tiles
    dma = pltpu.SemaphoreType.DMA
    f32, bf16 = jnp.float32, jnp.bfloat16
    mem = pltpu.VMEM
    chans = source.shape[1]
    block = (4, chans, 128)
    return pl.pallas_call(
        functools.partial(remap_kernel, faces, tiles),
        out_shape=(
            jax.ShapeDtypeStruct((count, chans, 128), bf16),
            jax.ShapeDtypeStruct((2,) + block, bf16),
            jax.ShapeDtypeStruct((2, chans, 128), bf16),
        ),
        in_specs=[SM, SM, VM, VM, VM, pl.BlockSpec(memory_space=pltpu.HBM)],
        out_specs=(VM, VM, VM),
        scratch_shapes=[
            mem(weight.shape, bf16),
            mem((count, chans, 128), bf16),
            mem((count, 32, 128), bf16),
            mem((count, 32, 128), bf16),
            mem((faces, tiles, 2, 128), jnp.int32),
            mem((count, 128), jnp.int32),
            mem((count, 128), jnp.int32),
            mem((count * 40 + 40, 128), f32),
            mem((count * 24 + 24, 128), f32),
            mem((count, chans, 128), bf16),
            mem((count, chans, 128), bf16),
            mem((2,) + block, bf16),
            mem(block, bf16),
            mem(block, bf16),
            mem((chans, 128), bf16),
            mem((tiles, chans, 128), bf16),
            mem((2,) + block, bf16),
            mem((4, chans, 512), f32),
            mem(block, bf16),
            mem((4,) + block, bf16),
            mem((faces,) + block, bf16),
            mem((faces,) + block, bf16),
            mem((faces,) + block, bf16),
            mem((2, 128), jnp.int32),
            mem((8, 128), jnp.int32),
            pltpu.SMEM((8, 128), jnp.int32),
            dma((4,)),
            dma, dma, dma, dma, dma, dma,
            dma((tiles,)), dma((tiles,)), dma((faces,)), dma((faces,)),
            dma((2,)), dma((2,)), dma((tiles,)), dma((tiles,)), dma((tiles,)), dma((2,)), dma((faces,)), dma((faces,)),
            dma((faces,)), dma((faces,)),
        ],
        compiler_params=pltpu.CompilerParams(
            collective_id=collective_id, has_side_effects=True, vmem_limit_bytes=VMEM_BYTES
        ),
    )(pick, links, entries, nested, source, weight)


def reduce_kernel(
    faces, tiles, wide_ref, one_ref, two_ref, ker_ref, grad_ref, first, part, second, mine, full, send_a, recv_a, send_b, recv_b,
    send_c, recv_c,
):
    face = lax.axis_index("face")
    tile = lax.axis_index("tile")
    f32, bf16 = jnp.float32, jnp.bfloat16
    size = wide_ref.shape[0] // tiles
    barrier = pltpu.get_barrier_semaphore()
    for k in range(1, tiles):
        pl.semaphore_signal(barrier, inc=1, device_id=(face, lax.rem(tile + k, tiles)), device_id_type=MESH)
    for k in range(1, faces):
        pl.semaphore_signal(barrier, inc=1, device_id=(lax.rem(face + k, faces), tile), device_id_type=MESH)
    grad_ref[...] = wide_ref[...].astype(bf16)
    pl.semaphore_wait(barrier, tiles + faces - 2)

    def spot(t):
        return pl.ds(pl.multiple_of(t * size, 16), size)

    copies = []
    for k in range(1, tiles):
        peer = lax.rem(tile + k, tiles)
        copies.append(
            pltpu.make_async_remote_copy(
                src_ref=grad_ref.at[spot(peer)],
                dst_ref=first.at[k],
                send_sem=send_a.at[k],
                recv_sem=recv_a.at[k],
                device_id=(face, peer),
                device_id_type=MESH,
            )
        )
        copies[-1].start()
    total = wide_ref[spot(tile), :]
    for k in range(1, tiles):
        copies[k - 1].wait_recv()
        total = total + first[k].astype(f32)
    part[...] = total.astype(bf16)
    second[face] = part[...]
    later = []
    for k in range(1, faces):
        later.append(
            pltpu.make_async_remote_copy(
                src_ref=part,
                dst_ref=second.at[face],
                send_sem=send_b.at[k],
                recv_sem=recv_b.at[k],
                device_id=(lax.rem(face + k, faces), tile),
                device_id_type=MESH,
            )
        )
        later[-1].start()
    for copy in later:
        copy.wait_recv()
    total = second[0].astype(f32)
    for k in range(1, faces):
        total = total + second[k].astype(f32)
    mine[...] = total.astype(bf16)
    full[spot(tile), :] = mine[...]
    last = []
    for k in range(1, tiles):
        last.append(
            pltpu.make_async_remote_copy(
                src_ref=mine,
                dst_ref=full.at[spot(tile)],
                send_sem=send_c.at[k],
                recv_sem=recv_c.at[k],
                device_id=(face, lax.rem(tile + k, tiles)),
                device_id_type=MESH,
            )
        )
        last[-1].start()
    for copy in last:
        copy.wait_recv()
    two_ref[...] = full[0:384, :].astype(f32).T[0:90, 0:360]
    one_ref[...] = full[384:768, :].astype(f32).T[0:90, 0:360]
    ker_ref[...] = full[368:384, 0:90].astype(f32)[0:9]
    for copy in copies + later + last:
        copy.wait_send()


def reduce_call(grad, collective_id):
    faces, tiles = lax.axis_size("face"), lax.axis_size("tile")
    dma = pltpu.SemaphoreType.DMA
    f32, bf16 = jnp.float32, jnp.bfloat16
    size = grad.shape[0] // tiles
    return pl.pallas_call(
        functools.partial(reduce_kernel, faces, tiles),
        out_shape=(
            jax.ShapeDtypeStruct((90, 360), f32),
            jax.ShapeDtypeStruct((90, 360), f32),
            jax.ShapeDtypeStruct((9, 90), f32),
        ),
        in_specs=[VM],
        out_specs=(VM, VM, VM),
        scratch_shapes=[
            pltpu.VMEM(grad.shape, bf16),
            pltpu.VMEM((tiles, size, 128), bf16),
            pltpu.VMEM((size, 128), bf16),
            pltpu.VMEM((faces, size, 128), bf16),
            pltpu.VMEM((size, 128), bf16),
            pltpu.VMEM(grad.shape, bf16),
            dma((tiles,)), dma((tiles,)), dma((faces,)), dma((faces,)), dma((tiles,)), dma((tiles,)),
        ],
        compiler_params=pltpu.CompilerParams(
            collective_id=collective_id, has_side_effects=True, vmem_limit_bytes=24 * MIB
        ),
    )(grad)


def remap(source, entry_block, entry_source, entry_weight, lat_to_nested, face_links):
    return remap_call(entry_source, face_links.transpose(2, 1, 0), entry_block[None], lat_to_nested[None], source, entry_weight, 1)

def per_device(
    source, entry_block, entry_source, entry_weight, lat_to_nested, face_links, w_in, b_in, kernel, ln_gain, ln_bias,
    w_one, b_one, w_two, b_two, cotangent,
):
    face_count = lax.axis_size("face")
    width = cotangent.shape[3]
    box, rows, cols = remap(source, entry_block, entry_source, entry_weight, lat_to_nested, face_links)
    scale = 1.0 / math.sqrt(face_count * width * width)
    output, grad = strip_call(
        box, rows, cols, cotangent[0], w_in, b_in, kernel, ln_gain, ln_bias, w_one, b_one, w_two, b_two,
        scale,
    )
    grad_one, grad_two, grad_kernel = reduce_call(grad, 4)
    return (output[None], grad_one, grad_two.T, grad_kernel)


def solution(mesh):
    split = P(("face", "tile"))
    strips = P("face", None, "tile", None)
    return jax.shard_map(
        per_device,
        mesh=mesh,
        in_specs=(split,) * 5 + (P(),) * 10 + (strips,),
        out_specs=(strips, P(), P(), P()),
        check_vma=False,
    )
```

```python
import functools
import math

import jax
import jax.numpy as jnp
from jax import lax
from jax.experimental import pallas as pl
from jax.experimental.pallas import tpu as pltpu
from jax.sharding import PartitionSpec as P


GELU_K = 0.7978845608028654
GELU_C = 0.044715
NORM_EPS = 1e-06
CP = 96
HP = 368
PITCH = 40
SLOTS = 4
MIB = 1024 * 1024


def strip_kernel(
    blocks_ref, rows_ref, cols_ref, cot_ref, win_ref, bin_ref, ker_ref, gain_ref, bias_ref, wone_ref,
    bone_ref, wtwo_ref, btwo_ref, out_ref, grad_ref, cot_v, out_v, field, cols, depth, back_d, turn_s, cot_t, out_t,
    scaled_s, norm_s, stds_s, pre_s, back_s, hid_s, bp_s, raw_s, g2_s, g1_s, gk_s, tab_s, vec_s, flat_s, w_in_s, w1t_s,
    w1_s, w2t_s, w2_s, sem_in, sem_out, scale,
):
    chans, rows, width = cot_ref.shape
    hidden = wone_ref.shape[1]
    lanes = width // 128
    f32, bf16 = jnp.float32, jnp.bfloat16
    nt = (((1,), (1,)), ((), ()))

    def wide(v):
        return jnp.concatenate([v] * lanes, axis=1)

    bring = pltpu.make_async_copy(cot_ref, cot_v, sem_in)
    bring.start()

    tab_s[...] = jnp.zeros_like(tab_s)
    for j, ref in enumerate((bin_ref, gain_ref, bias_ref, btwo_ref)):
        tab_s[j : j + 1, 0:chans] = ref[...]
    tab_s[4:13, 0:chans] = ker_ref[...]
    turned = tab_s[...].T
    for j in range(13):
        vec_s[j] = jnp.broadcast_to(turned[0:CP, j : j + 1], (CP, 128))
    tab_s[...] = jnp.zeros_like(tab_s)
    tab_s[0:16, 0:chans] = win_ref[...].astype(f32)
    w_in_s[...] = tab_s[...].T[0:CP, 0:16].astype(bf16)
    flat_s[...] = jnp.zeros_like(flat_s)
    flat_s[0:chans, 0:hidden] = wone_ref[...].astype(f32)
    w1_s[...] = flat_s[0:CP, 0:HP].astype(bf16)
    bone = bone_ref[0:1, 0:hidden]
    high = bone.astype(bf16).astype(f32)
    flat_s[chans : chans + 1, 0:hidden] = high
    flat_s[chans + 1 : chans + 2, 0:hidden] = bone - high
    w1t_s[...] = (flat_s[...].T[0:HP, 0:CP] * 0.5).astype(bf16)
    flat_s[...] = jnp.zeros_like(flat_s)
    flat_s[0:chans, 0:hidden] = wtwo_ref[...].astype(f32)
    w2t_s[...] = flat_s[0:CP, 0:HP].astype(bf16)
    w2_s[...] = (flat_s[...].T[0:HP, 0:CP] * 0.5).astype(bf16)

    tile, tile_count = lax.axis_index("tile"), lax.axis_size("tile")
    lane = lax.broadcasted_iota(jnp.int32, (CP, 128), 1)
    last = lane == jnp.where(tile == tile_count - 1, rows + 1, -1)
    first = lane == jnp.where(tile == 0, 0, -1)
    for side in range(2):
        v = jnp.dot(w_in_s[...], cols_ref[side], preferred_element_type=f32) + vec_s[0]
        cols[side] = jnp.where(first | last, 0.0, v.astype(bf16).astype(f32))

    g2_s[...] = jnp.zeros_like(g2_s)
    g1_s[...] = jnp.zeros_like(g1_s)
    def make_row(at, x):
        lat = jnp.dot(w_in_s[...], x, preferred_element_type=f32) + wide(vec_s[0])
        lat = lat.astype(bf16).astype(f32)
        wide_lane = lax.broadcasted_iota(jnp.int32, (CP, 128), 1)
        mid = [lat[:, k * 128 : (k + 1) * 128] for k in range(lanes)]
        up = [pltpu.roll(cols[0], lax.rem(128 - at, 128), 1)] + [pltpu.roll(m, 1, 1) for m in mid]
        dn = [pltpu.roll(m, 127, 1) for m in mid] + [pltpu.roll(cols[1], 127 - at, 1)]
        for k in range(lanes):
            part = slice(k * 128, (k + 1) * 128)
            field[at, 0, :, part] = jnp.where(wide_lane == 0, up[k], up[k + 1])
            field[at, 1, :, part] = mid[k]
            field[at, 2, :, part] = jnp.where(wide_lane == 127, dn[k + 1], dn[k])

    make_row(0, jnp.concatenate([rows_ref[0, k] for k in range(lanes)], axis=1))
    make_row(rows + 1, jnp.concatenate([rows_ref[1, k] for k in range(lanes)], axis=1))

    def row_step(r, _):
        make_row(r + 1, jnp.concatenate([blocks_ref[r * lanes + k] for k in range(lanes)], axis=1))
        return 0

    lax.fori_loop(0, rows, row_step, 0, unroll=8)

    bring.wait()
    turn_s[...] = jnp.zeros_like(turn_s)

    def turn(i, _):
        for j in range(16):
            c = i * 16 + j

            @pl.when(c < chans)
            def _():
                x = cot_v[c].astype(f32)
                for k in range(lanes):
                    turn_s[k, j * PITCH : j * PITCH + rows, :] = x[:, k * 128 : (k + 1) * 128]

        for r in range(rows):
            x = jnp.concatenate([turn_s[k, pl.ds(r, 16, stride=PITCH), :] for k in range(lanes)], axis=1)
            cot_t[r, pl.ds(pl.multiple_of(i * 16, 16), 16), :] = x.astype(bf16)
        return 0

    lax.fori_loop(0, CP // 16, turn, 0)

    def shifted(r, c):
        return [
            [field[r, side, pl.ds(c, 8), k * 128 : (k + 1) * 128] for k in range(lanes)] for side in range(3)
        ]

    def conv_chunk(i, _):
        c = pl.multiple_of(i * 8, 8)
        w = [vec_s[4 + tap, pl.ds(c, 8), :] for tap in range(9)]

        def mix(a, views, k):
            return w[3 * a] * views[0][k] + w[3 * a + 1] * views[1][k] + w[3 * a + 2] * views[2][k]

        v0, v1 = shifted(0, c), shifted(1, c)
        one = tuple(mix(0, v0, k) + mix(1, v1, k) for k in range(lanes))
        two = tuple(mix(0, v1, k) for k in range(lanes))

        def go(r, carry):
            one, two = carry
            v = shifted(r + 2, c)
            for k in range(lanes):
                depth[r, pl.ds(c, 8), k * 128 : (k + 1) * 128] = one[k] + mix(2, v, k)
            return (
                tuple(two[k] + mix(1, v, k) for k in range(lanes)),
                tuple(mix(0, v, k) for k in range(lanes)),
            )

        lax.fori_loop(0, rows, go, (one, two), unroll=16)
        return 0

    lax.fori_loop(0, CP // 8, conv_chunk, 0)

    row_id = lax.broadcasted_iota(jnp.int32, (CP, 128), 0)
    real = row_id < chans
    ones_rows = (row_id == chans) | (row_id == chans + 1)

    def col_sum(v):
        return jnp.sum(v, axis=0, keepdims=True)

    def norm_units(r, u):
        def unit(k):
            part = slice(k * 128, (k + 1) * 128)
            d = depth[r, :, part]
            d = d - col_sum(d) * (1.0 / chans)
            d = jnp.where(real, d, 0.0)
            inv_std = lax.rsqrt(col_sum(d * d) * (1.0 / chans) + NORM_EPS)
            s = d * inv_std
            at = lax.rem(r, 8)
            scaled_s[at, :, part] = s
            stds_s[at, :, part] = jnp.broadcast_to(inv_std, (8, 128))
            n = jnp.where(ones_rows, 1.0, s * vec_s[1] + vec_s[2])
            norm_s[u % 4, :, part] = n.astype(bf16)

        return [functools.partial(unit, k) for k in range(lanes)]

    halves = [slice(n, n + 256) for n in range(0, width, 256)]

    def widen_units(r, u):
        def pre(part):
            x = jnp.dot(w1t_s[...], norm_s[u % 4, :, part], preferred_element_type=f32)
            pre_s[u % 2, :, part] = x.astype(bf16)

        def back(part):
            x = jnp.dot(w2_s[...], cot_t[r, :, part], preferred_element_type=f32)
            back_s[u % 2, :, part] = x.astype(bf16)

        return [functools.partial(f, part) for part in halves for f in (pre, back)]

    def gelu_units(r, u):
        num = lambda v: jnp.asarray(v, bf16)

        def unit(h):
            x = pre_s[u % 2, h : h + 16, :]
            q = x * x
            t = jnp.tanh(x * (num(2.0 * GELU_K) + num(8.0 * GELU_K * GELU_C) * q))
            p = num(1.0) + t
            g = x * p
            slope = p + g * (num(1.0) - t) * (num(2.0 * GELU_K) + num(24.0 * GELU_K * GELU_C) * q)
            hid_s[u % 2, h : h + 16, :] = g
            bp_s[u % 2, h : h + 16, :] = back_s[u % 2, h : h + 16, :] * slope

        return [functools.partial(unit, h) for h in range(0, HP, 16)]

    def narrow_units(r, u):
        def out(part):
            raw_s[u % 2, 0, :, part] = jnp.dot(w2t_s[...], hid_s[u % 2, :, part], preferred_element_type=f32)

        def hat(part):
            raw_s[u % 2, 1, :, part] = jnp.dot(w1_s[...], bp_s[u % 2, :, part], preferred_element_type=f32)

        def two():
            g2_s[...] += lax.dot_general(hid_s[u % 2], cot_t[r], nt, preferred_element_type=f32)

        def one():
            g1_s[...] += lax.dot_general(bp_s[u % 2], norm_s[u % 4], nt, preferred_element_type=f32)

        units = [functools.partial(f, part) for part in halves for f in (out, hat)]
        return [units[0], units[1], two, units[2], units[3], one]

    def rear_units(r, u):
        def unit(k):
            part = slice(k * 128, (k + 1) * 128)
            at = lax.rem(r, 8)
            out_t[r, :, part] = (raw_s[u % 2, 0, :, part] + vec_s[3] + field[r + 1, 1, :, part]).astype(bf16)
            inv_std = stds_s[at, 0:1, part]
            b = raw_s[u % 2, 1, :, part] * vec_s[1]
            s = scaled_s[at, :, part]
            one = col_sum(b) * (inv_std * (1.0 / chans))
            two = col_sum(b * s) * (inv_std * (1.0 / chans))
            back_d[r, :, part] = b * inv_std - one - s * two

        return [functools.partial(unit, k) for k in range(lanes)]

    def beat(at, u, live):
        units = [
            make(at - s, u - s) if ok else []
            for s, (make, ok) in enumerate(zip((norm_units, widen_units, gelu_units, narrow_units, rear_units), live))
        ]
        vector = units[2]
        extra = units[0] + units[4]
        if extra and vector:
            gap = max(1, len(vector) // len(extra))
            mixed = []
            for i, v in enumerate(vector):
                mixed.append(v)
                if i % gap == gap - 1 and extra:
                    mixed.append(extra.pop(0))
            vector = mixed + extra
        else:
            vector = vector + extra
        matrix = []
        for i in range(max(len(units[1]), len(units[3]))):
            matrix += units[3][i : i + 1] + units[1][i : i + 1]
        share = len(vector) / max(1, len(matrix))
        done = 0
        for i, m in enumerate(matrix):
            m()
            upto = round((i + 1) * share)
            for v in vector[done:upto]:
                v()
            done = upto
        for v in vector[done:]:
            v()

    for at in range(4):
        beat(at, at, [at - s >= 0 for s in range(5)])

    def step(i, _):
        for u in range(SLOTS):
            beat(4 + i * SLOTS + u, 4 + u, [True] * 5)
        return 0

    lax.fori_loop(0, rows // SLOTS - 1, step, 0)
    for at in range(rows, rows + 4):
        beat(at, at, [at - s < rows for s in range(5)])

    def back(i, _):
        for r in range(rows):
            x = out_t[r, pl.ds(pl.multiple_of(i * 16, 16), 16), :].astype(f32)
            for k in range(lanes):
                turn_s[k, pl.ds(r, 16, stride=PITCH), :] = x[:, k * 128 : (k + 1) * 128]
        for j in range(16):
            c = i * 16 + j

            @pl.when(c < chans)
            def _():
                x = jnp.concatenate([turn_s[k, j * PITCH : j * PITCH + rows, :] for k in range(lanes)], axis=1)
                out_v[c] = x.astype(bf16)

        return 0

    lax.fori_loop(0, CP // 16, back, 0)
    take = pltpu.make_async_copy(out_v, out_ref, sem_out)
    take.start()

    def kernel_chunk(i, _):
        c = pl.multiple_of(i * 8, 8)

        def grad_row(r):
            return tuple(back_d[r, pl.ds(c, 8), k * 128 : (k + 1) * 128] for k in range(lanes))

        def fold(acc, a, b, views):
            new = list(acc)
            for s in range(3):
                m = b[0] * views[s][0]
                for k in range(1, lanes):
                    m = m + b[k] * views[s][k]
                new[3 * a + s] = new[3 * a + s] + m
            return tuple(new)

        acc = tuple(jnp.zeros((8, 128), f32) for _ in range(9))
        b0 = grad_row(0)
        acc = fold(acc, 0, b0, shifted(0, c))
        b1 = grad_row(1)
        v = shifted(1, c)
        acc = fold(fold(acc, 0, b1, v), 1, b0, v)

        def go(r, carry):
            acc, b1, b0 = carry
            v = shifted(r, c)
            b = grad_row(r)
            acc = fold(fold(fold(acc, 0, b, v), 1, b1, v), 2, b0, v)
            return acc, b, b1

        acc, b1, b0 = lax.fori_loop(2, rows, go, (acc, b1, b0), unroll=10)
        v = shifted(rows, c)
        acc = fold(fold(acc, 1, b1, v), 2, b0, v)
        acc = fold(acc, 2, b1, shifted(rows + 1, c))
        for tap in range(9):
            gk_s[tap, pl.ds(c, 8), :] = acc[tap]
        return 0

    lax.fori_loop(0, CP // 8, kernel_chunk, 0)
    grad_ref[360:384, :] = jnp.zeros((24, 128), f32)
    grad_ref[744:768, :] = jnp.zeros((24, 128), f32)
    grad_ref[0:hidden, 0:CP] = g2_s[0:hidden, :] * scale
    grad_ref[384 : 384 + hidden, 0:CP] = g1_s[0:hidden, :] * scale
    ones = jnp.ones((8, 128), f32)
    for tap in range(9):
        line = lax.dot_general(ones, gk_s[tap], nt, preferred_element_type=f32, precision=lax.Precision.HIGHEST)
        grad_ref[368 + tap : 369 + tap, 0:CP] = line[0:1, :] * scale
    take.wait()


def strip_call(blocks, rows, cols, cot, w_in, b_in, kernel, ln_gain, ln_bias, w_one, b_one, w_two, b_two, scale):
    chans, nrow, width = cot.shape
    f32, bf16 = jnp.float32, jnp.bfloat16
    lanes = width // 128
    vm = pl.BlockSpec(memory_space=pltpu.VMEM)
    hbm = pl.BlockSpec(memory_space=pltpu.HBM)
    mem = pltpu.VMEM
    return pl.pallas_call(
        functools.partial(strip_kernel, scale=scale),
        out_shape=(jax.ShapeDtypeStruct((chans, nrow, width), bf16), jax.ShapeDtypeStruct((768, 128), f32)),
        in_specs=[vm] * 3 + [hbm] + [vm] * 9,
        out_specs=(hbm, vm),
        scratch_shapes=[
            mem((chans, nrow, width), bf16),
            mem((chans, nrow, width), bf16),
            mem((nrow + 2, 3, CP, width), f32),
            mem((2, CP, 128), f32),
            mem((nrow, CP, width), f32),
            mem((nrow, CP, width), f32),
            mem((lanes, 17 * PITCH, 128), f32),
            mem((nrow, CP, width), bf16),
            mem((nrow, CP, width), bf16),
            mem((8, CP, width), f32),
            mem((4, CP, width), bf16),
            mem((8, 8, width), f32),
            mem((2, HP, width), bf16),
            mem((2, HP, width), bf16),
            mem((2, HP, width), bf16),
            mem((2, HP, width), bf16),
            mem((2, 2, CP, width), f32),
            mem((HP, CP), f32),
            mem((HP, CP), f32),
            mem((9, CP, 128), f32),
            mem((16, 128), f32),
            mem((13, CP, 128), f32),
            mem((128, 384), f32),
            mem((CP, 16), bf16),
            mem((HP, CP), bf16),
            mem((CP, HP), bf16),
            mem((CP, HP), bf16),
            mem((HP, CP), bf16),
            pltpu.SemaphoreType.DMA,
            pltpu.SemaphoreType.DMA,
        ],
        compiler_params=pltpu.CompilerParams(vmem_limit_bytes=60 * MIB),
    )(
        blocks, rows, cols, cot, w_in, b_in[None], kernel, ln_gain[None], ln_bias[None], w_one, jnp.pad(b_one, (0, 512 - b_one.shape[0]))[None],
        w_two.T, b_two[None],
    )


MESH = pl.DeviceIdType.MESH
MIB = 1024 * 1024
VMEM_BYTES = 60 * MIB
VM = pl.BlockSpec(memory_space=pltpu.VMEM)
SM = pl.BlockSpec(memory_space=pltpu.SMEM)
AXES = ("face", "tile")


def remap_kernel(
    faces, tiles, pick_ref, link_ref, entry_ref, nested_ref, source_ref, weight_ref, placed_ref, rows_ref, cols_ref, weight,
    part, box, got, table, block_of, nest_of, wide_s, narrow_s, box2, got2, edge, upper, lower, packet, packets, ends,
    line, wins, lots, chosen, windows, whole, ids, slot_v, slot_s, send_w, send_s, send_1, recv_1, local, send_2, recv_2, send_ia, recv_ia, send_ib, recv_ib,
    send_v, recv_v, send_p, recv_p, send_e, recv_e, send_n, recv_n, send_l, recv_l,
):
    f32, bf16 = jnp.float32, jnp.bfloat16
    face = lax.axis_index("face")
    tile = lax.axis_index("tile")
    count = faces * tiles
    me = face * tiles + tile
    chans = source_ref.shape[1]
    nrow = count // 4
    loads = weight_ref.shape[0] // 4

    def load(k):
        span = pl.ds(k * loads, loads)
        return pltpu.make_async_copy(weight_ref.at[span], weight.at[span], send_w.at[k])

    for k in range(4):
        load(k).start()
    barrier = pltpu.get_barrier_semaphore()

    def greet(k, _):
        peer = lax.rem(me + k, count)
        pl.semaphore_signal(barrier, inc=1, device_id=(peer // tiles, lax.rem(peer, tiles)), device_id_type=MESH)
        return 0

    lax.fori_loop(1, count, greet, 0)

    row = lax.broadcasted_iota(jnp.int32, (count, count), 0)
    col = lax.broadcasted_iota(jnp.int32, (count, count), 1)

    def turned(v):
        return jnp.broadcast_to(v, (count, count)).T

    ids[0:1, :] = entry_ref[...]
    ids[1:2, :] = nested_ref[...]
    hit = (jnp.broadcast_to(entry_ref[...], (count, count)) >> 7) == row
    fcol = col.astype(f32)
    low = turned(jnp.min(jnp.where(hit, fcol, float(count - 1)), axis=1, keepdims=True))
    high = turned(jnp.max(jnp.where(hit, fcol, 0.0), axis=1, keepdims=True))
    slot_v[...] = jnp.where(row[0:8] == 0, low[0:8], high[0:8]).astype(jnp.int32)
    to_scalars = pltpu.make_async_copy(slot_v, slot_s, send_s)
    to_scalars.start()

    group = 8
    for k in range(4):
        load(k).wait()

        def multiply(i, _):
            for j in range(group):
                e = k * loads + i * group + j
                x = jnp.dot(source_ref[pick_ref[e]], weight[e], preferred_element_type=f32)
                part[e] = x.astype(bf16)
            return 0

        lax.fori_loop(0, loads // group, multiply, 0)

    to_scalars.wait()

    def fill(d, _):
        box[d, 0:16, :] = part[slot_s[0, d] & (count - 1)]
        box[d, 16:32, :] = part[slot_s[1, d] & (count - 1)]
        return 0

    lax.fori_loop(0, count, fill, 0, unroll=8)
    table[face, tile] = ids[...]
    pl.semaphore_wait(barrier, count - 1)

    index = []
    for k in range(1, tiles):
        index.append(
            pltpu.make_async_remote_copy(
                src_ref=ids,
                dst_ref=table.at[face, tile],
                send_sem=send_ia.at[k],
                recv_sem=recv_ia.at[k],
                device_id=(face, lax.rem(tile + k, tiles)),
                device_id_type=MESH,
            )
        )
        index[-1].start()

    def exchange(src, dst, send, recv):
        def push(k, _):
            peer = lax.rem(me + k, count)
            pltpu.make_async_remote_copy(
                src_ref=src.at[peer],
                dst_ref=dst.at[me],
                send_sem=send,
                recv_sem=recv,
                device_id=(peer // tiles, lax.rem(peer, tiles)),
                device_id_type=MESH,
            ).start()
            return 0

        lax.fori_loop(1, count, push, 0, unroll=2)
        own = pltpu.make_async_copy(src.at[me], dst.at[me], local)
        own.start()
        return own

    def arrive(own, src, dst, recv):
        whole_box = pl.ds(0, count - 1)
        own.wait()
        pltpu.make_async_copy(src.at[whole_box], dst.at[whole_box], recv).wait()

    own = exchange(box, got, send_1, recv_1)
    for copy in index:
        copy.wait()
    index = []
    for k in range(1, faces):
        index.append(
            pltpu.make_async_remote_copy(
                src_ref=table.at[face],
                dst_ref=table.at[face],
                send_sem=send_ib.at[k],
                recv_sem=recv_ib.at[k],
                device_id=(lax.rem(face + k, faces), tile),
                device_id_type=MESH,
            )
        )
        index[-1].start()
    for copy in index:
        copy.wait()

    def spread(f, _):
        for t in range(tiles):
            pair = table[f, t]
            block_of[pl.ds(f * tiles + t, 1), :] = pair[0:1, :]
            nest_of[pl.ds(f * tiles + t, 1), :] = pair[1:2, :]
        return 0

    lax.fori_loop(0, faces, spread, 0)
    blocks = block_of[...]
    hit = (blocks >> 7) == me
    key = (col * count + (blocks & (count - 1))).astype(f32)
    low = jnp.min(jnp.where(hit, key, 1e9), axis=1, keepdims=True)
    high = jnp.max(jnp.where(hit, key, -1.0), axis=1, keepdims=True)
    low_label = jnp.where(high >= 0.0, low.astype(jnp.int32) & (count - 1), -1).astype(f32)
    high_label = jnp.where(high > low, high.astype(jnp.int32) & (count - 1), -1).astype(f32)
    nest = jnp.broadcast_to(nested_ref[...], (count, count))
    perm = jnp.sum(jnp.where((nest >> 7) == row, col.astype(f32), 0.0), axis=1, keepdims=True)
    take_low = (turned(low_label) == perm).astype(f32).astype(bf16)
    take_high = (turned(high_label) == perm).astype(f32).astype(bf16)
    nest = nest_of[...]
    spot = jnp.sum(jnp.where((nest >> 7) == me, (nest & (count - 1)).astype(f32), 0.0), axis=1, keepdims=True)
    place = (turned(spot) == row.astype(f32)).astype(f32).astype(bf16)

    arrive(own, box, got, recv_1)
    deep = 40

    def widen(s, _):
        wide_s[pl.ds(pl.multiple_of(s * deep, 8), 32), :] = got[s].astype(f32)
        return 0

    lax.fori_loop(0, count, widen, 0, unroll=8)
    pitch = 24
    for c in range(chans):
        one = wide_s[pl.ds(c, count, stride=deep), :].astype(bf16)
        two = wide_s[pl.ds(16 + c, count, stride=deep), :].astype(bf16)
        y = jnp.dot(take_low, one, preferred_element_type=f32) + jnp.dot(take_high, two, preferred_element_type=f32)
        narrow_s[pl.ds(c, count, stride=pitch), :] = y

    def narrow(d, _):
        box2[d] = narrow_s[pl.ds(pl.multiple_of(d * pitch, 8), 16), :].astype(bf16)
        return 0

    lax.fori_loop(0, count, narrow, 0, unroll=8)
    own = exchange(box2, got2, send_2, recv_2)
    arrive(own, box2, got2, recv_2)

    def widen_two(s, _):
        wide_s[pl.ds(pl.multiple_of(s * pitch, 8), 16), :] = got2[s].astype(f32)
        return 0

    lax.fori_loop(0, count, widen_two, 0, unroll=8)
    for c in range(chans):
        one = wide_s[pl.ds(c, count, stride=pitch), :].astype(bf16)
        narrow_s[pl.ds(c, count, stride=pitch), :] = jnp.dot(place, one, preferred_element_type=f32)

    def settle(m, _):
        placed_ref[m] = narrow_s[pl.ds(pl.multiple_of(m * pitch, 8), 16), :].astype(bf16)
        return 0

    lax.fori_loop(0, count, settle, 0, unroll=8)

    for k in range(4):
        edge[0, k] = placed_ref[k]
        edge[1, k] = placed_ref[4 * nrow - 4 + k]
    down = lax.rem(tile + 1, tiles)
    up = lax.rem(tile + tiles - 1, tiles)
    vertical = []
    for k, (dst, peer) in enumerate(((upper, down), (lower, up))):
        vertical.append(
            pltpu.make_async_remote_copy(
                src_ref=edge.at[1 - k],
                dst_ref=dst,
                send_sem=send_v.at[k],
                recv_sem=recv_v.at[k],
                device_id=(face, peer),
                device_id_type=MESH,
            )
        )
        vertical[-1].start()

    lane = lax.broadcasted_iota(jnp.int32, (chans, 128), 1)

    def pick(r, acc):
        left = pltpu.roll(placed_ref[4 * r].astype(f32), r, 1)
        right = pltpu.roll(placed_ref[4 * r + 3].astype(f32), r + nrow + 1, 1)
        return jnp.where(lane == r, left, jnp.where(lane == r + nrow, right, acc))

    packet[...] = lax.fori_loop(0, nrow, pick, jnp.zeros((chans, 128), f32), unroll=8).astype(bf16)
    packets[tile] = packet[...]
    sends = []
    for k in range(1, tiles):
        sends.append(
            pltpu.make_async_remote_copy(
                src_ref=packet,
                dst_ref=packets.at[tile],
                send_sem=send_p.at[k],
                recv_sem=recv_p.at[k],
                device_id=(face, lax.rem(tile + k, tiles)),
                device_id_type=MESH,
            )
        )
        sends[-1].start()
    def end_copy(k, side):
        return pltpu.make_async_remote_copy(
            src_ref=edge.at[side],
            dst_ref=ends.at[side],
            send_sem=send_e.at[k],
            recv_sem=recv_e.at[side],
            device_id=(face, lax.rem(tile + k, tiles)),
            device_id_type=MESH,
        )

    for side, owner in ((0, 0), (1, tiles - 1)):

        @pl.when(tile == owner)
        def _():
            for k in range(1, tiles):
                end_copy(k, side).start()
            ends[side] = edge[side]

    for copy in sends:
        copy.wait()
    for side, owner in ((0, 0), (1, tiles - 1)):

        @pl.when(tile == owner)
        def _():
            for k in range(1, tiles):
                end_copy(k, side).wait_send()

        @pl.when(tile != owner)
        def _():
            end_copy(1, side).wait_recv()

    per = 128 // nrow
    for side in range(2):
        line[side] = jnp.concatenate([ends[side, k] for k in range(4)], axis=1).astype(f32)
        parts = []
        for block in range(tiles // per):
            acc = jnp.zeros((chans, 128), f32)
            for i in range(per):
                seg = packets[block * per + i].astype(f32)
                seg = pltpu.roll(seg, (128 + (i - side) * nrow) % 128, 1) if i != side else seg
                acc = jnp.where((lane >= i * nrow) & (lane < (i + 1) * nrow), seg, acc)
            parts.append(acc)
        line[2 + side] = jnp.concatenate(parts, axis=1)
    width = tiles * nrow
    for s in range(4):
        full = line[s]
        near = pltpu.roll(full, lax.rem(width + 1 - tile * nrow, width), 1)[:, 0:128]
        far = pltpu.roll(full, lax.rem(width + 65 - (tiles - 1 - tile) * nrow, width), 1)[:, 0:128]
        wins[s] = jnp.where(lane < 64, near, far).astype(bf16)
    windows[face] = wins[...]
    sends = []
    for k in range(1, faces):
        sends.append(
            pltpu.make_async_remote_copy(
                src_ref=wins,
                dst_ref=windows.at[face],
                send_sem=send_n.at[k],
                recv_sem=recv_n.at[k],
                device_id=(lax.rem(face + k, faces), tile),
                device_id_type=MESH,
            )
        )
        sends[-1].start()

    def lot_copy(k):
        peer = lax.rem(face + k, faces)
        return pltpu.make_async_remote_copy(
            src_ref=chosen.at[k],
            dst_ref=whole.at[face],
            send_sem=send_l.at[k],
            recv_sem=recv_l.at[k],
            device_id=(peer, tile),
            device_id_type=MESH,
        )

    at_end = (tile == 0) | (tile == tiles - 1)
    end_side = jnp.where(tile == 0, 0, 1)

    @pl.when(at_end)
    def _():
        for s in range(4):
            for k in range(4):
                lots[s, k] = line[s, :, k * 128 : (k + 1) * 128].astype(bf16)
        for k in range(1, faces):
            chosen[k] = lots[link_ref[1, end_side, lax.rem(face + k, faces)]]
            lot_copy(k).start()

    for copy in vertical:
        copy.wait()
    for copy in sends:
        copy.wait()
    for side in range(2):
        view = windows[link_ref[0, 2 + side, face], link_ref[1, 2 + side, face]]
        spot = jnp.where(link_ref[2, 2 + side, face] == 1, 65 + nrow - col, col)
        turn = (row == spot).astype(bf16)
        cols_ref[side] = jnp.dot(view, turn, preferred_element_type=f32).astype(bf16)
        rows_ref[side] = (upper, lower)[side][...]

    @pl.when(at_end)
    def _():
        for k in range(1, faces):
            lot_copy(k).wait()

    for side, owner in ((0, 0), (1, tiles - 1)):

        @pl.when(tile == owner)
        def _():
            flip = link_ref[2, side, face] == 1
            turn = (row == jnp.where(flip, 127 - col, col)).astype(bf16)
            for k in range(4):
                view = whole[link_ref[0, side, face], jnp.where(flip, 3 - k, k)]
                rows_ref[side, k] = jnp.dot(view, turn, preferred_element_type=f32).astype(bf16)
    whole_box = pl.ds(0, count - 1)
    pltpu.make_async_copy(box.at[whole_box], got.at[whole_box], send_1).wait()
    pltpu.make_async_copy(box2.at[whole_box], got2.at[whole_box], send_2).wait()


def remap_call(pick, links, entries, nested, source, weight, collective_id):
    faces, tiles = lax.axis_size("face"), lax.axis_size("tile")
    count = faces * tiles
    dma = pltpu.SemaphoreType.DMA
    f32, bf16 = jnp.float32, jnp.bfloat16
    mem = pltpu.VMEM
    chans = source.shape[1]
    block = (4, chans, 128)
    return pl.pallas_call(
        functools.partial(remap_kernel, faces, tiles),
        out_shape=(
            jax.ShapeDtypeStruct((count, chans, 128), bf16),
            jax.ShapeDtypeStruct((2,) + block, bf16),
            jax.ShapeDtypeStruct((2, chans, 128), bf16),
        ),
        in_specs=[SM, SM, VM, VM, VM, pl.BlockSpec(memory_space=pltpu.HBM)],
        out_specs=(VM, VM, VM),
        scratch_shapes=[
            mem(weight.shape, bf16),
            mem((count, chans, 128), bf16),
            mem((count, 32, 128), bf16),
            mem((count, 32, 128), bf16),
            mem((faces, tiles, 2, 128), jnp.int32),
            mem((count, 128), jnp.int32),
            mem((count, 128), jnp.int32),
            mem((count * 40 + 40, 128), f32),
            mem((count * 24 + 24, 128), f32),
            mem((count, chans, 128), bf16),
            mem((count, chans, 128), bf16),
            mem((2,) + block, bf16),
            mem(block, bf16),
            mem(block, bf16),
            mem((chans, 128), bf16),
            mem((tiles, chans, 128), bf16),
            mem((2,) + block, bf16),
            mem((4, chans, 512), f32),
            mem(block, bf16),
            mem((4,) + block, bf16),
            mem((faces,) + block, bf16),
            mem((faces,) + block, bf16),
            mem((faces,) + block, bf16),
            mem((2, 128), jnp.int32),
            mem((8, 128), jnp.int32),
            pltpu.SMEM((8, 128), jnp.int32),
            dma((4,)),
            dma, dma, dma, dma, dma, dma,
            dma((tiles,)), dma((tiles,)), dma((faces,)), dma((faces,)),
            dma((2,)), dma((2,)), dma((tiles,)), dma((tiles,)), dma((tiles,)), dma((2,)), dma((faces,)), dma((faces,)),
            dma((faces,)), dma((faces,)),
        ],
        compiler_params=pltpu.CompilerParams(
            collective_id=collective_id, has_side_effects=True, vmem_limit_bytes=VMEM_BYTES
        ),
    )(pick, links, entries, nested, source, weight)


def reduce_kernel(
    faces, tiles, wide_ref, one_ref, two_ref, ker_ref, grad_ref, first, part, second, mine, full, send_a, recv_a, send_b, recv_b,
    send_c, recv_c,
):
    face = lax.axis_index("face")
    tile = lax.axis_index("tile")
    f32, bf16 = jnp.float32, jnp.bfloat16
    size = wide_ref.shape[0] // tiles
    barrier = pltpu.get_barrier_semaphore()
    for k in range(1, tiles):
        pl.semaphore_signal(barrier, inc=1, device_id=(face, lax.rem(tile + k, tiles)), device_id_type=MESH)
    for k in range(1, faces):
        pl.semaphore_signal(barrier, inc=1, device_id=(lax.rem(face + k, faces), tile), device_id_type=MESH)
    grad_ref[...] = wide_ref[...].astype(bf16)
    pl.semaphore_wait(barrier, tiles + faces - 2)

    def spot(t):
        return pl.ds(pl.multiple_of(t * size, 16), size)

    copies = []
    for k in range(1, tiles):
        peer = lax.rem(tile + k, tiles)
        copies.append(
            pltpu.make_async_remote_copy(
                src_ref=grad_ref.at[spot(peer)],
                dst_ref=first.at[k],
                send_sem=send_a.at[k],
                recv_sem=recv_a.at[k],
                device_id=(face, peer),
                device_id_type=MESH,
            )
        )
        copies[-1].start()
    total = wide_ref[spot(tile), :]
    for k in range(1, tiles):
        copies[k - 1].wait_recv()
        total = total + first[k].astype(f32)
    part[...] = total.astype(bf16)
    second[face] = part[...]
    later = []
    for k in range(1, faces):
        later.append(
            pltpu.make_async_remote_copy(
                src_ref=part,
                dst_ref=second.at[face],
                send_sem=send_b.at[k],
                recv_sem=recv_b.at[k],
                device_id=(lax.rem(face + k, faces), tile),
                device_id_type=MESH,
            )
        )
        later[-1].start()
    for copy in later:
        copy.wait_recv()
    total = second[0].astype(f32)
    for k in range(1, faces):
        total = total + second[k].astype(f32)
    mine[...] = total.astype(bf16)
    full[spot(tile), :] = mine[...]
    last = []
    for k in range(1, tiles):
        last.append(
            pltpu.make_async_remote_copy(
                src_ref=mine,
                dst_ref=full.at[spot(tile)],
                send_sem=send_c.at[k],
                recv_sem=recv_c.at[k],
                device_id=(face, lax.rem(tile + k, tiles)),
                device_id_type=MESH,
            )
        )
        last[-1].start()
    for copy in last:
        copy.wait_recv()
    two_ref[...] = full[0:384, :].astype(f32).T[0:90, 0:360]
    one_ref[...] = full[384:768, :].astype(f32).T[0:90, 0:360]
    ker_ref[...] = full[368:384, 0:90].astype(f32)[0:9]
    for copy in copies + later + last:
        copy.wait_send()


def reduce_call(grad, collective_id):
    faces, tiles = lax.axis_size("face"), lax.axis_size("tile")
    dma = pltpu.SemaphoreType.DMA
    f32, bf16 = jnp.float32, jnp.bfloat16
    size = grad.shape[0] // tiles
    return pl.pallas_call(
        functools.partial(reduce_kernel, faces, tiles),
        out_shape=(
            jax.ShapeDtypeStruct((90, 360), f32),
            jax.ShapeDtypeStruct((90, 360), f32),
            jax.ShapeDtypeStruct((9, 90), f32),
        ),
        in_specs=[VM],
        out_specs=(VM, VM, VM),
        scratch_shapes=[
            pltpu.VMEM(grad.shape, bf16),
            pltpu.VMEM((tiles, size, 128), bf16),
            pltpu.VMEM((size, 128), bf16),
            pltpu.VMEM((faces, size, 128), bf16),
            pltpu.VMEM((size, 128), bf16),
            pltpu.VMEM(grad.shape, bf16),
            dma((tiles,)), dma((tiles,)), dma((faces,)), dma((faces,)), dma((tiles,)), dma((tiles,)),
        ],
        compiler_params=pltpu.CompilerParams(
            collective_id=collective_id, has_side_effects=True, vmem_limit_bytes=24 * MIB
        ),
    )(grad)


def remap(source, entry_block, entry_source, entry_weight, lat_to_nested, face_links):
    return remap_call(entry_source, face_links.transpose(2, 1, 0), entry_block[None], lat_to_nested[None], source, entry_weight, 1)

def per_device(
    source, entry_block, entry_source, entry_weight, lat_to_nested, face_links, w_in, b_in, kernel, ln_gain, ln_bias,
    w_one, b_one, w_two, b_two, cotangent,
):
    face_count = lax.axis_size("face")
    width = cotangent.shape[3]
    box, rows, cols = remap(source, entry_block, entry_source, entry_weight, lat_to_nested, face_links)
    scale = 1.0 / math.sqrt(face_count * width * width)
    output, grad = strip_call(
        box, rows, cols, cotangent[0], w_in, b_in, kernel, ln_gain, ln_bias, w_one, b_one, w_two, b_two,
        scale,
    )
    grad_one, grad_two, grad_kernel = reduce_call(grad, 4)
    return (output[None], grad_one, grad_two.T, grad_kernel)


def solution(mesh):
    split = P(("face", "tile"))
    strips = P("face", None, "tile", None)
    return jax.shard_map(
        per_device,
        mesh=mesh,
        in_specs=(split,) * 5 + (P(),) * 10 + (strips,),
        out_specs=(strips, P(), P(), P()),
        check_vma=False,
    )
```
